32 devices in a mesh: band: 8 (over y, x, core), col: 4 (over z).
Axes of the slice: x: 2, y: 2, z: 4, core: 2. Of those that a mesh axis runs over, the one named last changes fastest.
Arguments:
- valence: bfloat16 [8, 128, 128, 128], P('band', 'col'), may hold values from -6 to 6
- conduction: bfloat16 [24, 128, 128, 128], P('band', 'col'), may hold values from -6 to 6
- energy_val: float32 [8], replicated, may hold values from -12 to -2
- energy_cond: float32 [24], P('band'), may hold values from 1 to 20
- kept: int32 [3, 1536], replicated, may hold values from 0 to 127
- plan: int32 [3], replicated, may hold values from 0 to 7
Outputs:
- response: float32 [1536, 1536], P('band', 'col')
The draws below stay inside these ranges and needn't reach their ends.
All inputs are finite; a program needn't handle non-finite values.
Results may differ from the reference program's by a relative error of at most 0.012.
Values may be sent and summed in bfloat16 or wider, within the bound.
No kernel may reach another device: no remote copies, remote signals or barrier semaphores. Data moves between devices by JAX's collectives and lax.ppermute only.
A program may use at most 192 MiB of HBM per device.

```python
import jax
import jax.numpy as jnp
from jax import lax

GRID = 128
KEEP = 1536
ROUNDS = 3
CBANDS = 24
VAL = 8


def place_ends(result, own_key, least, largest):
    longest = result.shape.index(max(result.shape))
    spots = []
    for shift in (0, 1):
        where = [jax.random.randint(jax.random.fold_in(own_key, axis), (), 0, length) for axis, length in enumerate(result.shape)]
        where[longest] = (where[longest] + shift) % result.shape[longest]
        spots.append(tuple(where))
    return result.at[spots[0]].set(least).at[spots[1]].set(largest)


def block_levels(key, extent, pieces, smallest, largest):
    def one(dim, blocks):
        draws = jax.random.uniform(jax.random.fold_in(jax.random.fold_in(key, 6), dim), (blocks,), jnp.float32, smallest / len(pieces), largest / len(pieces))
        return jnp.repeat(jnp.exp(draws), extent[dim] // blocks).reshape((-1,) + (1,) * (len(extent) - dim - 1))

    factor_of = one(*pieces[0])
    for cut in pieces[1:]:
        factor_of = factor_of * one(*cut)
    return factor_of


def scatter_about(stream_key, dims, width, reach, pieces=(), kind=jnp.bfloat16):
    factor_of = block_levels(stream_key, dims, pieces, -0.22, 0.18) if pieces else 1.0
    drawn = jax.random.normal(stream_key, dims, jnp.float32) * width * factor_of
    return jnp.minimum(jnp.maximum(drawn, -reach), reach).astype(kind)


def setup_inputs(seed: int = 0) -> dict:
    seeds = jax.random.split(jax.random.key(seed), 7)
    return {
        "valence": scatter_about(seeds[0], (VAL, GRID, GRID, GRID), 1.0, 6.0, ((0, 8), (1, 4))),
        "conduction": scatter_about(seeds[1], (CBANDS, GRID, GRID, GRID), 1.0, 6.0, ((0, 8), (1, 4))),
        "energy_val": jnp.clip(jax.random.uniform(seeds[2], (VAL,), jnp.float32, -12.0, -2.0), -12.0, -2.0),
        "energy_cond": jnp.clip(1.0 + 19.0 * jax.random.uniform(seeds[3], (CBANDS,), jnp.float32) ** block_levels(seeds[3], (CBANDS,), ((0, 8),), -0.2, 0.2), 1.0, 20.0),
        "kept": place_ends(jax.random.randint(seeds[4], (3, KEEP), 0, GRID), jax.random.fold_in(seeds[4], 1), 0, GRID - 1).astype(jnp.int32),
        "plan": jax.random.randint(seeds[5], (ROUNDS,), 0, VAL).astype(jnp.int32),
    }


def cas_table(frequency, position, length):
    phase_index = (frequency[:, None] * position[None, :]) % length
    angle_value = (2.0 * jnp.pi / length) * phase_index.astype(jnp.float32)
    return jnp.cos(angle_value) + jnp.sin(angle_value)


def reference(valence, conduction, energy_val, energy_cond, kept, plan):
    position = jnp.arange(GRID, dtype=jnp.int32)
    table_z = lax.optimization_barrier(cas_table(position, position, GRID).astype(jnp.bfloat16)).astype(jnp.float32)
    table_y = lax.optimization_barrier(cas_table(kept[1], position, GRID).astype(jnp.bfloat16)).astype(jnp.float32).T
    table_x = cas_table(kept[0], position, GRID).T
    norm_factor = GRID ** -1.5

    def pair_coeffs(valence_band, cond_band):
        product = (valence_band.astype(jnp.float32) * cond_band.astype(jnp.float32)).astype(jnp.bfloat16)
        product = lax.optimization_barrier(product).astype(jnp.float32)
        sectioned = jnp.dot(product.reshape(GRID * GRID, GRID), table_z, precision=lax.Precision.HIGHEST)
        sectioned = lax.optimization_barrier(sectioned.astype(jnp.bfloat16)).astype(jnp.float32)
        sectioned = sectioned.reshape(GRID, GRID, GRID)
        picked = jnp.take(sectioned, kept[2], axis=2)
        along_y = jnp.einsum("xyq,yq->xq", picked, table_y, precision=lax.Precision.HIGHEST)
        return jnp.sum(along_y * table_x, axis=0) * norm_factor

    def one_round(target):
        valence_band = lax.dynamic_index_in_dim(valence, target, 0, keepdims=False)
        coeffs = lax.map(lambda cond_band: pair_coeffs(valence_band, cond_band), conduction)
        weights = 1.0 / (energy_cond - energy_val[target])
        return coeffs, weights

    coeffs, weights = lax.map(one_round, plan)
    coeffs = coeffs.reshape(ROUNDS * CBANDS, KEEP)
    weights = weights.reshape(ROUNDS * CBANDS)
    plain_coeffs = coeffs.astype(jnp.bfloat16)
    weighted = (weights[:, None] * coeffs).astype(jnp.bfloat16)
    summed = lax.dot_general(weighted, plain_coeffs, (((0,), (0,)), ((), ())), preferred_element_type=jnp.float32)
    return -summed * ((ROUNDS * CBANDS) ** -0.5)
```

```python
import jax
import jax.numpy as jnp
from jax import lax
from jax.experimental import pallas as pl
from jax.experimental.pallas import tpu as pltpu
from jax.sharding import PartitionSpec as P

LANES = 128
NT = (((1,), (1,)), ((), ()))


def cas_of(phase, length):
    angle_value = 2.0 * jnp.pi / length * phase.astype(jnp.float32)
    return jnp.cos(angle_value) + jnp.sin(angle_value)


def round_kernel(index_ref, va_ref, vb_ref, c0_ref, c1_ref, table_ref, tx_ref, out_ref, s_ref, a_ref, g_ref):
    half, length = va_ref.shape[0], va_ref.shape[1]
    bands = c0_ref.shape[0]
    planes = 2 * half
    lanes = tx_ref.shape[1]
    keep = tx_ref.shape[0]
    table = table_ref[...]

    def transform_z(c_ref, band_base):
        def step(i, carry):
            band, x = i // half, (i % half) * 2
            in_a = x < half
            xa = jnp.minimum(x, half - 2)
            xb = jnp.maximum(x - half, 0)
            v = jnp.where(in_a, va_ref[pl.ds(xa, 2)], vb_ref[pl.ds(xb, 2)])
            product = (v * c_ref[band, pl.ds(x, 2)]).reshape(2 * length, length)
            out = lax.dot_general(table, product, NT, preferred_element_type=jnp.float32)
            out = out.astype(jnp.bfloat16).astype(jnp.float32)
            row = (band_base + band) * planes + x
            s_ref[pl.ds(row, length, stride=lanes), :] = out[:, :length]
            s_ref[pl.ds(row + 1, length, stride=lanes), :] = out[:, length:]
            return carry

        lax.fori_loop(0, bands * half, step, 0, unroll=4)

    transform_z(c0_ref, 0)
    transform_z(c1_ref, bands)

    def transform_y(j, carry):
        rows = s_ref[pl.ds(pl.multiple_of(j * 2 * lanes, 2 * lanes), 2 * lanes), :].astype(jnp.bfloat16)
        out = lax.dot_general(table, rows, NT, preferred_element_type=jnp.float32)
        base = pl.multiple_of(j * 2 * length, 2 * length)
        a_ref[pl.ds(base, length), :] = out[:, :lanes]
        a_ref[pl.ds(base + length, length), :] = out[:, lanes:]
        return carry

    lax.fori_loop(0, length // 2, transform_y, 0, unroll=4)

    def pick(q, carry):
        g_ref[pl.ds(q, 1), :] = a_ref[pl.ds(index_ref[q], 1), :]
        return carry

    lax.fori_loop(0, keep, pick, 0, unroll=16)

    used = 2 * bands * planes
    lane = lax.broadcasted_iota(jnp.int32, (keep, lanes), 1)
    scaled = jnp.where(lane < used, g_ref[...] * tx_ref[...], 0.0)
    high = scaled.astype(jnp.bfloat16)
    low = (scaled - high.astype(jnp.float32)).astype(jnp.bfloat16)
    rows = out_ref.shape[0]
    owner = lax.broadcasted_iota(jnp.int32, (rows, lanes), 1) // planes
    select = (owner == lax.broadcasted_iota(jnp.int32, (rows, lanes), 0)).astype(jnp.bfloat16)
    out_ref[...] = lax.dot_general(select, high, NT, preferred_element_type=jnp.float32) + lax.dot_general(
        select, low, NT, preferred_element_type=jnp.float32
    )


def round_coeffs(index, va, vb, c0, c1, table, tx):
    keep, lanes = tx.shape
    length = table.shape[0]
    rows = -(-2 * c0.shape[0] // 8) * 8
    vmem = pl.BlockSpec(memory_space=pltpu.VMEM)
    return pl.pallas_call(
        round_kernel,
        out_shape=jax.ShapeDtypeStruct((rows, keep), jnp.float32),
        in_specs=[pl.BlockSpec(memory_space=pltpu.SMEM)] + [vmem] * 6,
        out_specs=vmem,
        scratch_shapes=[
            pltpu.VMEM((length * lanes, length), jnp.float32),
            pltpu.VMEM((length * length, lanes), jnp.float32),
            pltpu.VMEM((keep, lanes), jnp.float32),
        ],
        compiler_params=pltpu.CompilerParams(vmem_limit_bytes=30 * 2**20),
        cost_estimate=pl.CostEstimate(flops=4 * 10**9, bytes_accessed=12 * 2**20, transcendentals=0),
        name="round_coeffs",
    )(index, va, vb, c0, c1, table, tx)


def per_device(valence, conduction, energy_val, energy_cond, kept, plan):
    band_local, x_local, length = conduction.shape[:3]
    keep = kept.shape[1]
    held = valence.shape[0]
    rounds = plan.shape[0]
    n_band = lax.axis_size("band")
    n_col = lax.axis_size("col")
    n_pair = n_band // 2
    bits = n_pair.bit_length() - 1
    me = lax.axis_index("band")
    side, group = me % 2, me // 2
    col = lax.axis_index("col")
    x_half = x_local // 2

    def swap(value, mask):
        return lax.ppermute(value, "band", [(i, i ^ mask) for i in range(n_band)])

    def halves(value):
        low, high = value[:, :x_half], value[:, x_half:]
        return jnp.where(side == 0, low, high), jnp.where(side == 0, high, low)

    v_mine, v_other = halves(valence)
    v_swapped = swap(v_other, 1)
    c_mine, c_other = halves(conduction)
    c_swapped = swap(c_other, 1)
    c0 = jnp.where(side == 0, c_mine, c_swapped)
    c1 = jnp.where(side == 0, c_swapped, c_mine)

    root = plan // held
    local = plan % held
    relative = (root // 2) ^ group
    root_side = root % 2

    def slot(values, r):
        return lax.dynamic_index_in_dim(values, local[r], 0, keepdims=False)

    def spread(mine, swapped, order):
        if 2 * held <= rounds and order:
            bit = order[0]
            far_mine, far_swapped = swap(jnp.concatenate([mine, swapped]), 2 << bit).reshape(2, *mine.shape)
            slots = []
            for r in range(rounds):
                same = root_side[r] == side
                near = jnp.where(same, slot(mine, r), slot(swapped, r))
                far = jnp.where(same, slot(far_mine, r), slot(far_swapped, r))
                slots.append(jnp.where((relative[r] >> bit) & 1 == 0, near, far))
            order = order[1:]
        else:
            slots = [jnp.where(root_side[r] == side, slot(mine, r), slot(swapped, r)) for r in range(rounds)]
        for bit in order:
            far = [swap(s, 2 << bit) for s in slots]
            slots = [jnp.where((relative[r] >> bit) & 1 == 0, slots[r], far[r]) for r in range(rounds)]
        return slots

    cut = x_half // 2
    part_a = spread(v_mine[:, :cut], v_swapped[:, :cut], list(range(bits)))
    part_b = spread(v_mine[:, cut:], v_swapped[:, cut:], list(range(bits))[::-1])

    position = jnp.arange(length, dtype=jnp.int32)
    table = cas_of(position[:, None] * position[None, :] % length, length).astype(jnp.bfloat16)
    used = 2 * band_local * x_half
    lanes = -(-used // LANES) * LANES
    x_global = col * x_local + side * x_half + jnp.arange(lanes, dtype=jnp.int32) % x_half
    tx = cas_of(kept[0][:, None] * x_global[None, :] % length, length) * length ** (-1.5)
    index = kept[2] * length + kept[1]

    partial = [round_coeffs(index, part_a[r], part_b[r], c0, c1, table, tx) for r in range(rounds)]

    first = jnp.concatenate([p[:band_local] for p in partial])
    second = jnp.concatenate([p[band_local : 2 * band_local] for p in partial])
    mine = jnp.where(side == 0, first, second)
    coeffs = mine + swap(jnp.where(side == 0, second, first), 1)
    sent = coeffs.astype(jnp.bfloat16)
    for shift in range(1, n_col):
        moved = lax.ppermute(sent, "col", [(i, (i + shift) % n_col) for i in range(n_col)])
        coeffs = coeffs + moved.astype(jnp.float32)
    weights = jnp.concatenate([1.0 / (energy_cond - energy_val[plan[r]]) for r in range(rounds)])
    weighted = (weights[:, None] * coeffs).astype(jnp.bfloat16)
    plain = coeffs.astype(jnp.bfloat16)

    col_width, row_width = keep // n_col, keep // n_band
    col_piece = lax.dynamic_slice_in_dim(plain, col * col_width, col_width, 1)

    def rows_of(other):
        return lax.dynamic_slice_in_dim(weighted, other * 2 * row_width, 2 * row_width, 1)

    pieces = [jnp.concatenate([col_piece, rows_of(group)], axis=1)]
    for mask in range(1, n_pair):
        pieces.append(swap(jnp.concatenate([col_piece, rows_of(group ^ mask)], axis=1), 2 * mask))
    gathered = jnp.concatenate(pieces)
    columns = gathered[:, :col_width]
    rows_low, rows_high = gathered[:, col_width : col_width + row_width], gathered[:, col_width + row_width :]
    rows_mine = jnp.where(side == 0, rows_low, rows_high)
    rows_other = jnp.where(side == 0, rows_high, rows_low)
    swapped = swap(jnp.concatenate([columns, rows_other], axis=1), 1)
    columns = jnp.concatenate([columns, swapped[:, :col_width]])
    rows = jnp.concatenate([rows_mine, swapped[:, col_width:]])
    response_tile = lax.dot_general(
        rows, columns, (((0,), (0,)), ((), ())), preferred_element_type=jnp.float32
    )
    factor = (rounds * band_local * n_band) ** (-0.5)
    return -response_tile * factor


def solution(mesh):
    return jax.shard_map(
        per_device,
        mesh=mesh,
        in_specs=(
            P("band", "col", None, None),
            P("band", "col", None, None),
            P(),
            P("band"),
            P(),
            P(),
        ),
        out_specs=P("band", "col"),
        check_vma=False,
    )
```

```python
import jax
import jax.numpy as jnp
from jax import lax
from jax.experimental import pallas as pl
from jax.experimental.pallas import tpu as pltpu
from jax.sharding import PartitionSpec as P

LANES = 128
NT = (((1,), (1,)), ((), ()))


def cas_of(phase, length):
    angle_value = 2.0 * jnp.pi / length * phase.astype(jnp.float32)
    return jnp.cos(angle_value) + jnp.sin(angle_value)


def spaced_rows(used):
    tiles = -(-used // 8)
    return 8 * (tiles + 1 - tiles % 2)


def round_kernel(index_ref, va_ref, vb_ref, c0_ref, c1_ref, table_ref, tx_ref, out_ref, s_ref, a_ref, g_ref):
    length = va_ref.shape[1]
    bands = c0_ref.shape[0]
    planes = c0_ref.shape[1]
    keep, lanes = tx_ref.shape
    used = 2 * bands * planes
    spaced = spaced_rows(used)
    table = table_ref[...]

    def transform_z(c_ref, v_ref, band_base, x_base):
        half = v_ref.shape[0]
        steps = half // 2

        def step(i, carry):
            band, x = i // steps, (i % steps) * 2
            product = (v_ref[pl.ds(x, 2)] * c_ref[band, pl.ds(x + x_base, 2)]).reshape(2 * length, length)
            out = lax.dot_general(table, product, NT, preferred_element_type=jnp.float32)
            out = out.astype(jnp.bfloat16).astype(jnp.float32)
            row = (band_base + band) * planes + x + x_base
            s_ref[pl.ds(row, length, stride=spaced), :] = out[:, :length]
            s_ref[pl.ds(row + 1, length, stride=spaced), :] = out[:, length:]
            return carry

        lax.fori_loop(0, bands * steps, step, 0, unroll=bands * steps)

    for c_ref, band_base in ((c0_ref, 0), (c1_ref, bands)):
        transform_z(c_ref, va_ref, band_base, 0)
        transform_z(c_ref, vb_ref, band_base, va_ref.shape[0])

    def transform_y(j, carry):
        base = pl.multiple_of(j * 2 * spaced, 8)
        rows = jnp.concatenate([s_ref[pl.ds(base, lanes), :], s_ref[pl.ds(base + spaced, lanes), :]])
        out = lax.dot_general(table, rows.astype(jnp.bfloat16), NT, preferred_element_type=jnp.float32)
        base = pl.multiple_of(j * 2 * length, 2 * length)
        a_ref[pl.ds(base, length), :] = out[:, :lanes]
        a_ref[pl.ds(base + length, length), :] = out[:, lanes:]
        return carry

    lax.fori_loop(0, length // 2, transform_y, 0, unroll=16)

    def pick(t, carry):
        rows = [a_ref[pl.ds(index_ref[t * 8 + k], 1), :] for k in range(8)]
        g_ref[pl.ds(pl.multiple_of(t * 8, 8), 8), :] = jnp.concatenate(rows)
        return carry

    lax.fori_loop(0, keep // 8, pick, 0, unroll=8)

    lane = lax.broadcasted_iota(jnp.int32, (keep, lanes), 1)
    scaled = jnp.where(lane < used, g_ref[...] * tx_ref[...], 0.0)
    high = scaled.astype(jnp.bfloat16)
    low = (scaled - high.astype(jnp.float32)).astype(jnp.bfloat16)
    rows = out_ref.shape[0]
    owner = lax.broadcasted_iota(jnp.int32, (rows, lanes), 1) // planes
    select = (owner == lax.broadcasted_iota(jnp.int32, (rows, lanes), 0)).astype(jnp.bfloat16)
    out_ref[...] = lax.dot_general(select, high, NT, preferred_element_type=jnp.float32) + lax.dot_general(
        select, low, NT, preferred_element_type=jnp.float32
    )


def round_coeffs(index, va, vb, c0, c1, table, tx):
    keep, lanes = tx.shape
    length = table.shape[0]
    rows = -(-2 * c0.shape[0] // 8) * 8
    vmem = pl.BlockSpec(memory_space=pltpu.VMEM)
    return pl.pallas_call(
        round_kernel,
        out_shape=jax.ShapeDtypeStruct((rows, keep), jnp.float32),
        in_specs=[pl.BlockSpec(memory_space=pltpu.SMEM)] + [vmem] * 6,
        out_specs=vmem,
        scratch_shapes=[
            pltpu.VMEM((length * spaced_rows(2 * c0.shape[0] * c0.shape[1]) + lanes, length), jnp.float32),
            pltpu.VMEM((length * length, lanes), jnp.float32),
            pltpu.VMEM((keep, lanes), jnp.float32),
        ],
        compiler_params=pltpu.CompilerParams(vmem_limit_bytes=32 * 2**20),
        cost_estimate=pl.CostEstimate(flops=4 * 10**9, bytes_accessed=12 * 2**20, transcendentals=0),
        name="round_coeffs",
    )(index, va, vb, c0, c1, table, tx)


def per_device(valence, conduction, energy_val, energy_cond, kept, plan):
    band_local, x_local, length = conduction.shape[:3]
    keep = kept.shape[1]
    held = valence.shape[0]
    rounds = plan.shape[0]
    n_band = lax.axis_size("band")
    n_col = lax.axis_size("col")
    n_pair = n_band // 2
    bits = n_pair.bit_length() - 1
    me = lax.axis_index("band")
    side, group = me % 2, me // 2
    col = lax.axis_index("col")
    x_half = x_local // 2

    def swap(value, mask):
        return lax.ppermute(value, "band", [(i, i ^ mask) for i in range(n_band)])

    def half_of(value, which):
        return lax.dynamic_slice_in_dim(value, which * x_half, x_half, 1)

    v_mine = half_of(valence, side)
    v_swapped = swap(half_of(valence, 1 - side), 1)
    c_mine = half_of(conduction, side)
    c_swapped = swap(half_of(conduction, 1 - side), 1)

    position = jnp.arange(length, dtype=jnp.int32)
    table = cas_of(position[:, None] * position[None, :] % length, length).astype(jnp.bfloat16)
    used = 2 * band_local * x_half
    lanes = -(-used // LANES) * LANES
    x_global = col * x_local + side * x_half + jnp.arange(lanes, dtype=jnp.int32) % x_half
    tx = cas_of(kept[0][:, None] * x_global[None, :] % length, length) * length ** (-1.5)
    index = kept[2] * length + kept[1]

    is_target = plan[:, None] == jnp.arange(energy_val.shape[0], dtype=jnp.int32)[None, :]
    target_energy = jnp.sum(jnp.where(is_target, energy_val[None, :], 0.0), axis=1)
    weights = (1.0 / (energy_cond[None, :] - target_energy[:, None])).reshape(rounds * band_local, 1)

    plan_rows = jnp.broadcast_to(plan[:, None, None, None], (rounds, 1, 1, length))
    root = plan_rows // held
    local = plan_rows % held
    relative = (root // 2) ^ group
    near_side = root % 2 == side

    def held_band(mine, swapped, r):
        band = jnp.where(near_side[r], mine[0], swapped[0])
        for i in range(1, held):
            band = jnp.where(local[r] == i, jnp.where(near_side[r], mine[i], swapped[i]), band)
        return band

    def nearer(r, bit, near, far):
        return jnp.where((relative[r] >> bit) & 1 == 0, near, far)

    cut = x_half // 2
    parts = [(v_mine[:, :cut], v_swapped[:, :cut]), (v_mine[:, cut:], v_swapped[:, cut:])]
    orders = [list(range(bits)), list(range(bits))[::-1]]
    if 2 * held <= rounds and bits:
        far_mine = [swap(part[0], 2 << order[0]) for part, order in zip(parts, orders)]
        far_swapped = [swap(part[1], 2 << order[0]) for part, order in zip(parts, orders)]
        far_mine, far_swapped, c_swapped, table, tx, index, weights = lax.optimization_barrier(
            (far_mine, far_swapped, c_swapped, table, tx, index, weights)
        )
        slots = [
            [nearer(r, order[0], held_band(*part, r), held_band(fm, fs, r)) for part, fm, fs, order in zip(parts, far_mine, far_swapped, orders)]
            for r in range(rounds)
        ]
        slots = lax.optimization_barrier(slots)
        orders = [order[1:] for order in orders]
    else:
        slots = [[held_band(*part, r) for part in parts] for r in range(rounds)]
    for step in range(len(orders[0])):
        slots = [
            [nearer(r, order[step], value, swap(value, 2 << order[step])) for value, order in zip(slots[r], orders)]
            for r in range(rounds)
        ]

    c0 = jnp.where(side == 0, c_mine, c_swapped)
    c1 = jnp.where(side == 0, c_swapped, c_mine)

    partial = [round_coeffs(index, *slots[r], c0, c1, table, tx) for r in range(rounds)]

    first = jnp.concatenate([p[:band_local] for p in partial])
    second = jnp.concatenate([p[band_local : 2 * band_local] for p in partial])
    mine = jnp.where(side == 0, first, second)
    coeffs = mine + swap(jnp.where(side == 0, second, first), 1)
    sent = coeffs.astype(jnp.bfloat16)
    for shift in range(1, n_col):
        moved = lax.ppermute(sent, "col", [(i, (i + shift) % n_col) for i in range(n_col)])
        coeffs = coeffs + moved.astype(jnp.float32)
    weighted = (weights * coeffs).astype(jnp.bfloat16)
    plain = coeffs.astype(jnp.bfloat16)

    col_width, row_width = keep // n_col, keep // n_band
    col_piece = lax.dynamic_slice_in_dim(plain, col * col_width, col_width, 1)

    def rows_of(other):
        return lax.dynamic_slice_in_dim(weighted, other * 2 * row_width, 2 * row_width, 1)

    pieces = [jnp.concatenate([col_piece, rows_of(group)], axis=1)]
    for mask in range(1, n_pair):
        pieces.append(swap(jnp.concatenate([col_piece, rows_of(group ^ mask)], axis=1), 2 * mask))
    gathered = jnp.concatenate(pieces)
    columns = gathered[:, :col_width]
    rows_low, rows_high = gathered[:, col_width : col_width + row_width], gathered[:, col_width + row_width :]
    rows_mine = jnp.where(side == 0, rows_low, rows_high)
    rows_other = jnp.where(side == 0, rows_high, rows_low)
    swapped = swap(jnp.concatenate([columns, rows_other], axis=1), 1)
    columns = jnp.concatenate([columns, swapped[:, :col_width]])
    rows = jnp.concatenate([rows_mine, swapped[:, col_width:]])
    response_tile = lax.dot_general(
        rows, columns, (((0,), (0,)), ((), ())), preferred_element_type=jnp.float32
    )
    factor = (rounds * band_local * n_band) ** (-0.5)
    return -response_tile * factor


def solution(mesh):
    return jax.shard_map(
        per_device,
        mesh=mesh,
        in_specs=(
            P("band", "col", None, None),
            P("band", "col", None, None),
            P(),
            P("band"),
            P(),
            P(),
        ),
        out_specs=P("band", "col"),
        check_vma=False,
    )
```

```python
import jax
import jax.numpy as jnp
from jax import lax
from jax.experimental import pallas as pl
from jax.experimental.pallas import tpu as pltpu
from jax.sharding import PartitionSpec as P

LANES = 128
NT = (((1,), (1,)), ((), ()))


def cas_of(phase, length):
    angle_value = 2.0 * jnp.pi / length * phase.astype(jnp.float32)
    return jnp.cos(angle_value) + jnp.sin(angle_value)


def spaced_rows(used):
    tiles = -(-used // 8)
    return 8 * (tiles + 1 - tiles % 2)


def round_kernel(index_ref, va_ref, vb_ref, c0_ref, c1_ref, table_ref, tx_ref, out_ref, s_ref, a_ref, g_ref):
    length = va_ref.shape[1]
    bands = c0_ref.shape[0]
    planes = c0_ref.shape[1]
    keep, lanes = tx_ref.shape
    used = 2 * bands * planes
    spaced = spaced_rows(used)
    table = table_ref[...]

    def transform_z(c_ref, v_ref, band_base, x_base):
        half = v_ref.shape[0]
        steps = half // 2

        def step(i, carry):
            band, x = i // steps, (i % steps) * 2
            product = (v_ref[pl.ds(x, 2)] * c_ref[band, pl.ds(x + x_base, 2)]).reshape(2 * length, length)
            out = lax.dot_general(table, product, NT, preferred_element_type=jnp.float32)
            out = out.astype(jnp.bfloat16).astype(jnp.float32)
            row = (band_base + band) * planes + x + x_base
            s_ref[pl.ds(row, length, stride=spaced), :] = out[:, :length]
            s_ref[pl.ds(row + 1, length, stride=spaced), :] = out[:, length:]
            return carry

        lax.fori_loop(0, bands * steps, step, 0, unroll=bands * steps)

    for c_ref, band_base in ((c0_ref, 0), (c1_ref, bands)):
        transform_z(c_ref, va_ref, band_base, 0)
        transform_z(c_ref, vb_ref, band_base, va_ref.shape[0])

    def transform_y(j, carry):
        base = pl.multiple_of(j * 2 * spaced, 8)
        rows = jnp.concatenate([s_ref[pl.ds(base, lanes), :], s_ref[pl.ds(base + spaced, lanes), :]])
        out = lax.dot_general(table, rows.astype(jnp.bfloat16), NT, preferred_element_type=jnp.float32)
        base = pl.multiple_of(j * 2 * length, 2 * length)
        a_ref[pl.ds(base, length), :] = out[:, :lanes]
        a_ref[pl.ds(base + length, length), :] = out[:, lanes:]
        return carry

    lax.fori_loop(0, length // 2, transform_y, 0, unroll=16)

    def pick(t, carry):
        rows = [a_ref[pl.ds(index_ref[t * 8 + k], 1), :] for k in range(8)]
        g_ref[pl.ds(pl.multiple_of(t * 8, 8), 8), :] = jnp.concatenate(rows)
        return carry

    lax.fori_loop(0, keep // 8, pick, 0, unroll=8)

    lane = lax.broadcasted_iota(jnp.int32, (keep, lanes), 1)
    scaled = jnp.where(lane < used, g_ref[...] * tx_ref[...], 0.0)
    high = scaled.astype(jnp.bfloat16)
    low = (scaled - high.astype(jnp.float32)).astype(jnp.bfloat16)
    rows = out_ref.shape[0]
    owner = lax.broadcasted_iota(jnp.int32, (rows, lanes), 1) // planes
    select = (owner == lax.broadcasted_iota(jnp.int32, (rows, lanes), 0)).astype(jnp.bfloat16)
    out_ref[...] = lax.dot_general(select, high, NT, preferred_element_type=jnp.float32) + lax.dot_general(
        select, low, NT, preferred_element_type=jnp.float32
    )


def round_coeffs(index, va, vb, c0, c1, table, tx):
    keep, lanes = tx.shape
    length = table.shape[0]
    rows = -(-2 * c0.shape[0] // 8) * 8
    vmem = pl.BlockSpec(memory_space=pltpu.VMEM)
    return pl.pallas_call(
        round_kernel,
        out_shape=jax.ShapeDtypeStruct((rows, keep), jnp.float32),
        in_specs=[pl.BlockSpec(memory_space=pltpu.SMEM)] + [vmem] * 6,
        out_specs=vmem,
        scratch_shapes=[
            pltpu.VMEM((length * spaced_rows(2 * c0.shape[0] * c0.shape[1]) + lanes, length), jnp.float32),
            pltpu.VMEM((length * length, lanes), jnp.float32),
            pltpu.VMEM((keep, lanes), jnp.float32),
        ],
        compiler_params=pltpu.CompilerParams(vmem_limit_bytes=24 * 2**20),
        cost_estimate=pl.CostEstimate(flops=4 * 10**9, bytes_accessed=12 * 2**20, transcendentals=0),
        name="round_coeffs",
    )(index, va, vb, c0, c1, table, tx)


def per_device(valence, conduction, energy_val, energy_cond, kept, plan):
    band_local, x_local, length = conduction.shape[:3]
    keep = kept.shape[1]
    held = valence.shape[0]
    rounds = plan.shape[0]
    n_band = lax.axis_size("band")
    n_col = lax.axis_size("col")
    n_pair = n_band // 2
    bits = n_pair.bit_length() - 1
    me = lax.axis_index("band")
    side, group = me % 2, me // 2
    col = lax.axis_index("col")
    x_half = x_local // 2

    def swap(value, mask):
        return lax.ppermute(value, "band", [(i, i ^ mask) for i in range(n_band)])

    def half_of(value, which):
        return lax.dynamic_slice_in_dim(value, which * x_half, x_half, 1)

    cut = x_half // 2
    part_starts = (0, cut)

    def parts_of(which):
        return [lax.dynamic_slice_in_dim(valence, which * x_half + start, cut, 1) for start in part_starts]

    v_swapped = [swap(part, 1) for part in parts_of(1 - side)]
    v_mine = parts_of(side)
    v_swapped, conduction, kept, plan, energy_val = lax.optimization_barrier(
        (v_swapped, conduction, kept, plan, energy_val)
    )
    c_mine = half_of(conduction, side)
    c_swapped = swap(half_of(conduction, 1 - side), 1)

    position = jnp.arange(length, dtype=jnp.int32)
    table = cas_of(position[:, None] * position[None, :] % length, length).astype(jnp.bfloat16)
    used = 2 * band_local * x_half
    lanes = -(-used // LANES) * LANES
    x_global = col * x_local + side * x_half + jnp.arange(lanes, dtype=jnp.int32) % x_half
    tx = cas_of(kept[0][:, None] * x_global[None, :] % length, length) * length ** (-1.5)
    index = kept[2] * length + kept[1]

    is_target = plan[:, None] == jnp.arange(energy_val.shape[0], dtype=jnp.int32)[None, :]
    target_energy = jnp.sum(jnp.where(is_target, energy_val[None, :], 0.0), axis=1)
    weights = (1.0 / (energy_cond[None, :] - target_energy[:, None])).reshape(rounds * band_local, 1)

    plan_rows = jnp.broadcast_to(plan[:, None, None, None], (rounds, 1, 1, length))
    root = plan_rows // held
    local = plan_rows % held
    relative = (root // 2) ^ group
    near_side = root % 2 == side

    def held_band(mine, swapped, r):
        band = jnp.where(near_side[r], mine[0], swapped[0])
        for i in range(1, held):
            band = jnp.where(local[r] == i, jnp.where(near_side[r], mine[i], swapped[i]), band)
        return band

    def nearer(r, bit, near, far):
        return jnp.where((relative[r] >> bit) & 1 == 0, near, far)

    parts = list(zip(v_mine, v_swapped))
    orders = [list(range(bits)), list(range(bits))[::-1]]
    if 2 * held <= rounds and bits:
        far_mine = [swap(part[0], 2 << order[0]) for part, order in zip(parts, orders)]
        far_swapped = [swap(part[1], 2 << order[0]) for part, order in zip(parts, orders)]
        far_mine, far_swapped, c_swapped, table, tx, index, weights = lax.optimization_barrier(
            (far_mine, far_swapped, c_swapped, table, tx, index, weights)
        )
        slots = [
            [nearer(r, order[0], held_band(*part, r), held_band(fm, fs, r)) for part, fm, fs, order in zip(parts, far_mine, far_swapped, orders)]
            for r in range(rounds)
        ]
        slots = lax.optimization_barrier(slots)
        orders = [order[1:] for order in orders]
    else:
        slots = [[held_band(*part, r) for part in parts] for r in range(rounds)]
    for step in range(len(orders[0])):
        slots = [
            [nearer(r, order[step], value, swap(value, 2 << order[step])) for value, order in zip(slots[r], orders)]
            for r in range(rounds)
        ]

    c0 = jnp.where(side == 0, c_mine, c_swapped)
    c1 = jnp.where(side == 0, c_swapped, c_mine)

    partial = [round_coeffs(index, *slots[r], c0, c1, table, tx) for r in range(rounds)]

    first = jnp.concatenate([p[:band_local] for p in partial])
    second = jnp.concatenate([p[band_local : 2 * band_local] for p in partial])
    mine = jnp.where(side == 0, first, second)
    coeffs = mine + swap(jnp.where(side == 0, second, first), 1)
    sent = coeffs.astype(jnp.bfloat16)
    for shift in range(1, n_col):
        moved = lax.ppermute(sent, "col", [(i, (i + shift) % n_col) for i in range(n_col)])
        coeffs = coeffs + moved.astype(jnp.float32)
    weighted = (weights * coeffs).astype(jnp.bfloat16)
    plain = coeffs.astype(jnp.bfloat16)

    col_width, row_width = keep // n_col, keep // n_band
    col_piece = lax.dynamic_slice_in_dim(plain, col * col_width, col_width, 1)

    def rows_of(other):
        return lax.dynamic_slice_in_dim(weighted, other * 2 * row_width, 2 * row_width, 1)

    pieces = [jnp.concatenate([col_piece, rows_of(group)], axis=1)]
    for mask in range(1, n_pair):
        pieces.append(swap(jnp.concatenate([col_piece, rows_of(group ^ mask)], axis=1), 2 * mask))
    gathered = jnp.concatenate(pieces)
    columns = gathered[:, :col_width]
    rows_low, rows_high = gathered[:, col_width : col_width + row_width], gathered[:, col_width + row_width :]
    rows_mine = jnp.where(side == 0, rows_low, rows_high)
    rows_other = jnp.where(side == 0, rows_high, rows_low)
    swapped = swap(jnp.concatenate([columns, rows_other], axis=1), 1)
    columns = jnp.concatenate([columns, swapped[:, :col_width]])
    rows = jnp.concatenate([rows_mine, swapped[:, col_width:]])
    response_tile = lax.dot_general(
        rows, columns, (((0,), (0,)), ((), ())), preferred_element_type=jnp.float32
    )
    factor = (rounds * band_local * n_band) ** (-0.5)
    return -response_tile * factor


def solution(mesh):
    return jax.shard_map(
        per_device,
        mesh=mesh,
        in_specs=(
            P("band", "col", None, None),
            P("band", "col", None, None),
            P(),
            P("band"),
            P(),
            P(),
        ),
        out_specs=P("band", "col"),
        check_vma=False,
    )
```

```python
import jax
import jax.numpy as jnp
from jax import lax
from jax.experimental import pallas as pl
from jax.experimental.pallas import tpu as pltpu
from jax.sharding import PartitionSpec as P

LANES = 128
NT = (((1,), (1,)), ((), ()))


def cas_of(phase, length):
    angle_value = 2.0 * jnp.pi / length * phase.astype(jnp.float32)
    return jnp.cos(angle_value) + jnp.sin(angle_value)


def spaced_rows(used):
    tiles = -(-used // 8)
    return 8 * (tiles + 1 - tiles % 2)


def round_kernel(index_ref, va_ref, vb_ref, c0_ref, c1_ref, table_ref, tx_ref, out_ref, s_ref, a_ref, g_ref):
    length = va_ref.shape[1]
    bands = c0_ref.shape[0]
    planes = c0_ref.shape[1]
    keep, lanes = tx_ref.shape
    used = 2 * bands * planes
    spaced = spaced_rows(used)
    table = table_ref[...]

    def transform_z(c_ref, v_ref, band_base, x_base):
        half = v_ref.shape[0]
        steps = half // 2

        def step(i, carry):
            band, x = i // steps, (i % steps) * 2
            product = (v_ref[pl.ds(x, 2)] * c_ref[band, pl.ds(x + x_base, 2)]).reshape(2 * length, length)
            out = lax.dot_general(table, product, NT, preferred_element_type=jnp.float32)
            out = out.astype(jnp.bfloat16).astype(jnp.float32)
            row = (band_base + band) * planes + x + x_base
            s_ref[pl.ds(row, length, stride=spaced), :] = out[:, :length]
            s_ref[pl.ds(row + 1, length, stride=spaced), :] = out[:, length:]
            return carry

        lax.fori_loop(0, bands * steps, step, 0, unroll=bands * steps)

    for c_ref, band_base in ((c0_ref, 0), (c1_ref, bands)):
        transform_z(c_ref, va_ref, band_base, 0)
        transform_z(c_ref, vb_ref, band_base, va_ref.shape[0])

    def transform_y(j, carry):
        base = pl.multiple_of(j * 2 * spaced, 8)
        rows = jnp.concatenate([s_ref[pl.ds(base, lanes), :], s_ref[pl.ds(base + spaced, lanes), :]])
        out = lax.dot_general(table, rows.astype(jnp.bfloat16), NT, preferred_element_type=jnp.float32)
        base = pl.multiple_of(j * 2 * length, 2 * length)
        a_ref[pl.ds(base, length), :] = out[:, :lanes]
        a_ref[pl.ds(base + length, length), :] = out[:, lanes:]
        return carry

    lax.fori_loop(0, length // 2, transform_y, 0, unroll=16)

    def pick(t, carry):
        rows = [a_ref[pl.ds(index_ref[t * 8 + k], 1), :] for k in range(8)]
        g_ref[pl.ds(pl.multiple_of(t * 8, 8), 8), :] = jnp.concatenate(rows)
        return carry

    lax.fori_loop(0, keep // 8, pick, 0, unroll=8)

    lane = lax.broadcasted_iota(jnp.int32, (keep, lanes), 1)
    scaled = jnp.where(lane < used, g_ref[...] * tx_ref[...], 0.0)
    high = scaled.astype(jnp.bfloat16)
    low = (scaled - high.astype(jnp.float32)).astype(jnp.bfloat16)
    rows = out_ref.shape[0]
    owner = lax.broadcasted_iota(jnp.int32, (rows, lanes), 1) // planes
    select = (owner == lax.broadcasted_iota(jnp.int32, (rows, lanes), 0)).astype(jnp.bfloat16)
    out_ref[...] = lax.dot_general(select, high, NT, preferred_element_type=jnp.float32) + lax.dot_general(
        select, low, NT, preferred_element_type=jnp.float32
    )


def round_coeffs(index, va, vb, c0, c1, table, tx):
    keep, lanes = tx.shape
    length = table.shape[0]
    rows = -(-2 * c0.shape[0] // 8) * 8
    vmem = pl.BlockSpec(memory_space=pltpu.VMEM)
    return pl.pallas_call(
        round_kernel,
        out_shape=jax.ShapeDtypeStruct((rows, keep), jnp.float32),
        in_specs=[pl.BlockSpec(memory_space=pltpu.SMEM)] + [vmem] * 6,
        out_specs=vmem,
        scratch_shapes=[
            pltpu.VMEM((length * spaced_rows(2 * c0.shape[0] * c0.shape[1]) + lanes, length), jnp.float32),
            pltpu.VMEM((length * length, lanes), jnp.float32),
            pltpu.VMEM((keep, lanes), jnp.float32),
        ],
        compiler_params=pltpu.CompilerParams(vmem_limit_bytes=18 * 2**20),
        cost_estimate=pl.CostEstimate(flops=4 * 10**9, bytes_accessed=12 * 2**20, transcendentals=0),
        name="round_coeffs",
    )(index, va, vb, c0, c1, table, tx)


def square_kernel(plan_ref, energy_val_ref, energy_cond_ref, flag_ref, weight_ref):
    rounds, bands = plan_ref.shape[0], energy_cond_ref.shape[0]
    me = lax.axis_index("band")
    side, group = me & 1, me >> 1
    plan = [plan_ref[r] for r in range(rounds)]

    def one(condition):
        return jnp.where(condition, 1, 0)

    def relative_of(band):
        return (band >> 1) ^ group

    at, own_side, repeated = jnp.int32(-1), jnp.int32(0), []
    for r in range(rounds):
        others = [plan[i] for i in range(rounds) if i != r]
        double = sum(one(band == (plan[r] ^ 1)) for band in others) > 0
        repeated.append(sum(one(band == plan[r]) for band in others) > 0)
        at = jnp.where(double, relative_of(plan[r]), at)
        own_side = jnp.where(relative_of(plan[r]) == 0, plan[r] & 1, own_side)

    def early_of(band):
        relative, low = relative_of(band), band & 1
        at_x = jnp.where(at == 1, 1 - low, 1)
        at_y = jnp.where(at == 2, low, 1)
        return jnp.where(relative == 0, 1, jnp.where(relative == 1, at_x, jnp.where(relative == 2, at_y, 0)))

    first, best = jnp.int32(0), jnp.int32(-1)
    for r in range(rounds):
        score = jnp.where(early_of(plan[r]) == 1, 2, one(repeated[r]))
        first = jnp.where(score > best, r, first)
        best = jnp.maximum(score, best)
    ordered = [plan[0]] + [jnp.where(first == r, plan[0], plan[r]) for r in range(1, rounds)]
    for r in range(1, rounds):
        ordered[0] = jnp.where(first == r, plan[r], ordered[0])

    own_double = one(at == 0)
    flags = [
        own_double,
        one(jnp.where(at == 0, 0, own_side) == side),
        one(jnp.where(at == 0, 1, own_side) == side),
        one(at >= 0),
        early_of(ordered[0]),
    ]
    for band in ordered:
        relative, low = relative_of(band), band & 1
        y_at_3 = jnp.where(at == 3, 1 - low, one(at == 1))
        x_at_3 = jnp.where(at == 3, low, one(at == 2))
        from_x = jnp.where(relative == 1, jnp.where(at == 1, low, 0), jnp.where(relative == 3, x_at_3, 0))
        from_y = jnp.where(relative == 2, jnp.where(at == 2, 1 - low, 0), jnp.where(relative == 3, y_at_3, 0))
        flags += [
            one(relative == 1),
            one(relative == 2),
            one((band & 1) == side),
            from_x,
            from_y,
            jnp.where(relative == 3, one(at <= 0), 0),
            one(band == ordered[0]),
        ]
    for k, flag in enumerate(flags):
        flag_ref[pl.ds(k, 1), :] = jnp.full((1, LANES), flag, jnp.int32)
    for r in range(rounds):
        for c in range(bands):
            gap = energy_cond_ref[c] - energy_val_ref[ordered[r]]
            weight_ref[pl.ds(r * bands + c, 1), :] = 1.0 / jnp.full((1, LANES), gap, jnp.float32)


def square_flags(plan, energy_val, energy_cond):
    rounds = plan.shape[0]
    smem = pl.BlockSpec(memory_space=pltpu.SMEM)
    vmem = pl.BlockSpec(memory_space=pltpu.VMEM)
    count = -(-(5 + 7 * rounds) // 8) * 8
    weight_rows = -(-rounds * energy_cond.shape[0] // 8) * 8
    return pl.pallas_call(
        square_kernel,
        out_shape=(
            jax.ShapeDtypeStruct((count, LANES), jnp.int32),
            jax.ShapeDtypeStruct((weight_rows, LANES), jnp.float32),
        ),
        in_specs=[smem] * 3,
        out_specs=(vmem, vmem),
        name="square_flags",
    )(plan, energy_val, energy_cond)


def per_device(valence, conduction, energy_val, energy_cond, kept, plan):
    band_local, x_local, length = conduction.shape[:3]
    keep = kept.shape[1]
    held = valence.shape[0]
    rounds = plan.shape[0]
    n_band = lax.axis_size("band")
    n_col = lax.axis_size("col")
    n_pair = n_band // 2
    bits = n_pair.bit_length() - 1
    me = lax.axis_index("band")
    side, group = me % 2, me // 2
    col = lax.axis_index("col")
    x_half = x_local // 2

    def swap(value, mask):
        return lax.ppermute(value, "band", [(i, i ^ mask) for i in range(n_band)])

    def half_of(value, which):
        return lax.dynamic_slice_in_dim(value, which * x_half, x_half, 1)

    cut = x_half // 2
    part_starts = (0, cut)

    def parts_of(which):
        return [lax.dynamic_slice_in_dim(valence, which * x_half + start, cut, 1) for start in part_starts]

    v_mine = parts_of(side)
    v_swapped = [swap(part, 1) for part in parts_of(1 - side)]
    square = held == 1 and bits == 2 and rounds > 1
    flags, square_weights = square_flags(plan, energy_val, energy_cond) if square else (plan, energy_val)
    v_swapped, conduction, flags = lax.optimization_barrier((v_swapped, conduction, flags))
    c_swapped = swap(half_of(conduction, 1 - side), 1)

    def prepared(conduction, kept):
        c_mine = half_of(conduction, side)
        position = jnp.arange(length, dtype=jnp.int32)
        table = cas_of(position[:, None] * position[None, :] % length, length).astype(jnp.bfloat16)
        used = 2 * band_local * x_half
        lanes = -(-used // LANES) * LANES
        x_global = col * x_local + side * x_half + jnp.arange(lanes, dtype=jnp.int32) % x_half
        tx = cas_of(kept[0][:, None] * x_global[None, :] % length, length) * length ** (-1.5)
        index = kept[2] * length + kept[1]
        c0 = jnp.where(side == 0, c_mine, c_swapped)
        c1 = jnp.where(side == 0, c_swapped, c_mine)
        return c0, c1, table, tx, index

    def coeffs_of(pair, c0, c1, table, tx, index):
        return round_coeffs(index, *pair, c0, c1, table, tx)

    def located(plan):
        plan_rows = jnp.broadcast_to(plan[:, None, None, None], (rounds, 1, 1, length))
        root = plan_rows // held
        return (root // 2) ^ group, root % 2 == side, plan_rows % held

    parts = list(zip(v_mine, v_swapped))

    def any_plan():
        relative, near_side, local = located(plan)
        ready = prepared(conduction, kept)
        is_target = plan[:, None] == jnp.arange(energy_val.shape[0], dtype=jnp.int32)[None, :]
        target_energy = jnp.sum(jnp.where(is_target, energy_val[None, :], 0.0), axis=1)
        weights = (1.0 / (energy_cond[None, :] - target_energy[:, None])).reshape(rounds * band_local, 1)

        def held_band(mine, swapped, r):
            band = jnp.where(near_side[r], mine[0], swapped[0])
            for i in range(1, held):
                band = jnp.where(local[r] == i, jnp.where(near_side[r], mine[i], swapped[i]), band)
            return band

        def nearer(r, bit, near, far):
            return jnp.where((relative[r] >> bit) & 1 == 0, near, far)

        orders = [list(range(bits)), list(range(bits))[::-1]]
        if 2 * held <= rounds and bits:
            far_mine = [swap(part[0], 2 << order[0]) for part, order in zip(parts, orders)]
            far_swapped = [swap(part[1], 2 << order[0]) for part, order in zip(parts, orders)]
            far_mine, far_swapped, ready = lax.optimization_barrier((far_mine, far_swapped, ready))
            slots = [
                [
                    nearer(r, order[0], held_band(*part, r), held_band(fm, fs, r))
                    for part, fm, fs, order in zip(parts, far_mine, far_swapped, orders)
                ]
                for r in range(rounds)
            ]
            slots = lax.optimization_barrier(slots)
            orders = [order[1:] for order in orders]
        else:
            slots = [[held_band(*part, r) for part in parts] for r in range(rounds)]
        for step in range(len(orders[0])):
            slots = [
                [nearer(r, order[step], value, swap(value, 2 << order[step])) for value, order in zip(slots[r], orders)]
                for r in range(rounds)
            ]
        return [coeffs_of(pair, *ready) for pair in slots], weights

    def four_pairs(flags, weights):
        def flag(k):
            return flags[k] != 0

        def round_flag(r, k):
            return flag(5 + 7 * r + k)

        def own(k):
            return [jnp.where(flag(k), part[0][0], part[1][0]) for part in parts]

        to_x, to_y = own(1), own(2)
        to_x, to_y, *given = lax.optimization_barrier((to_x, to_y, conduction, kept))
        x_a, y_b = swap(to_x[0], 2), swap(to_y[1], 4)
        x_b, y_a = swap(to_x[1], 2), swap(to_y[0], 4)
        ready = prepared(*given)
        x_a, y_b, ready = lax.optimization_barrier((x_a, y_b, ready))
        on_y, on_x = jnp.where(flag(0), to_x[0], x_a), jnp.where(flag(0), to_y[1], y_b)
        on_y, on_x, flags = lax.optimization_barrier((on_y, on_x, flags))
        on_y, on_x = swap(on_y, 4), swap(on_x, 2)

        def near(r, half, x, y):
            here = jnp.where(round_flag(r, 2), parts[half][0][0], parts[half][1][0])
            return jnp.where(round_flag(r, 0), x, jnp.where(round_flag(r, 1), y, here))

        partial = [coeffs_of((near(0, 0, x_a, y_a), near(0, 1, x_b, y_b)), *ready)]
        partial, on_x, on_y, flags = lax.optimization_barrier((partial, on_x, on_y, flags))
        later_x, later_y = jnp.where(flag(0), to_y[0], y_a), jnp.where(flag(0), to_x[1], x_b)
        last_x, last_y = lax.cond(
            flags[3, 0] != 0,
            lambda x, y: (swap(x, 2), swap(y, 4)),
            lambda x, y: (x, y),
            later_x,
            later_y,
        )
        for r in range(1, rounds):
            from_x, from_y, from_both = (round_flag(r, k) for k in (3, 4, 5))
            part_a = jnp.where(from_x, last_x, jnp.where(from_y | from_both, on_y, near(r, 0, x_a, y_a)))
            part_b = jnp.where(from_y, last_y, jnp.where(from_x | from_both, on_x, near(r, 1, x_b, y_b)))
            partial.append(coeffs_of((part_a, part_b), *ready))
        copied = partial[rounds - 1]
        for r in range(1, rounds - 1):
            copied = jnp.where(flags[5 + 7 * r + 6, :1] != 0, partial[r], copied)
        partial[0] = jnp.where(flags[4, :1] != 0, partial[0], copied)
        return partial, weights[: rounds * band_local, :1]

    partial, weights = four_pairs(flags, square_weights) if square else any_plan()

    first = jnp.concatenate([p[:band_local] for p in partial])
    second = jnp.concatenate([p[band_local : 2 * band_local] for p in partial])
    mine = jnp.where(side == 0, first, second)
    coeffs = mine + swap(jnp.where(side == 0, second, first), 1)
    sent = coeffs.astype(jnp.bfloat16)
    for shift in range(1, n_col):
        moved = lax.ppermute(sent, "col", [(i, (i + shift) % n_col) for i in range(n_col)])
        coeffs = coeffs + moved.astype(jnp.float32)
    weighted = (weights * coeffs).astype(jnp.bfloat16)
    plain = coeffs.astype(jnp.bfloat16)

    col_width, row_width = keep // n_col, keep // n_band
    col_piece = lax.dynamic_slice_in_dim(plain, col * col_width, col_width, 1)

    def rows_of(other):
        return lax.dynamic_slice_in_dim(weighted, other * 2 * row_width, 2 * row_width, 1)

    pieces = [jnp.concatenate([col_piece, rows_of(group)], axis=1)]
    for mask in range(1, n_pair):
        pieces.append(swap(jnp.concatenate([col_piece, rows_of(group ^ mask)], axis=1), 2 * mask))
    gathered = jnp.concatenate(pieces)
    columns = gathered[:, :col_width]
    rows_low, rows_high = gathered[:, col_width : col_width + row_width], gathered[:, col_width + row_width :]
    rows_mine = jnp.where(side == 0, rows_low, rows_high)
    rows_other = jnp.where(side == 0, rows_high, rows_low)
    swapped = swap(jnp.concatenate([columns, rows_other], axis=1), 1)
    columns = jnp.concatenate([columns, swapped[:, :col_width]])
    rows = jnp.concatenate([rows_mine, swapped[:, col_width:]])
    response_tile = lax.dot_general(
        rows, columns, (((0,), (0,)), ((), ())), preferred_element_type=jnp.float32
    )
    factor = (rounds * band_local * n_band) ** (-0.5)
    return -response_tile * factor


def solution(mesh):
    return jax.shard_map(
        per_device,
        mesh=mesh,
        in_specs=(
            P("band", "col", None, None),
            P("band", "col", None, None),
            P(),
            P("band"),
            P(),
            P(),
        ),
        out_specs=P("band", "col"),
        check_vma=False,
    )
```

```python
import functools

import jax
import jax.numpy as jnp
from jax import lax
from jax.experimental import pallas as pl
from jax.experimental.pallas import tpu as pltpu
from jax.sharding import PartitionSpec as P

LANES = 128
NT = (((1,), (1,)), ((), ()))


def cas_of(phase, length):
    angle_value = 2.0 * jnp.pi / length * phase.astype(jnp.float32)
    return jnp.cos(angle_value) + jnp.sin(angle_value)


def spaced_rows(used):
    tiles = -(-used // 8)
    return 8 * (tiles + 1 - tiles % 2)


def round_kernel(choices, place, pick_ref, index_ref, *refs):
    table_ref, conduction_ref, swapped_ref, tx_from, out_ref, va_ref, vb_ref, c_ref, tx_ref, s_ref, a_ref, g_ref, sem_ref = refs[
        2 * choices :
    ]
    bands, planes = swapped_ref.shape[:2]
    side = lax.axis_index("band") & 1
    parts = [(refs[:choices], va_ref), (refs[choices : 2 * choices], vb_ref)]
    for part, (sources, target) in enumerate(parts):
        for k, source in enumerate(sources):

            @pl.when(pick_ref[2 * place + part] == k)
            def _():
                pltpu.make_async_copy(source, target, sem_ref.at[part]).start()

    for band in range(bands):
        mine, other = side * bands + band, (1 - side) * bands + band
        own_planes = conduction_ref.at[band, pl.ds(side * planes, planes)]
        pltpu.make_async_copy(own_planes, c_ref.at[mine], sem_ref.at[2 + mine]).start()
        pltpu.make_async_copy(swapped_ref.at[band], c_ref.at[other], sem_ref.at[2 + other]).start()
    tx_copy = pltpu.make_async_copy(tx_from, tx_ref, sem_ref.at[2 + 2 * bands])
    tx_copy.start()
    for part, (sources, target) in enumerate(parts):
        pltpu.make_async_copy(sources[0], target, sem_ref.at[part]).wait()
    length = va_ref.shape[1]
    keep, lanes = tx_ref.shape
    used = 2 * bands * planes
    spaced = spaced_rows(used)
    table = table_ref[...]

    def transform_z(band, v_ref, x_base):
        steps = v_ref.shape[0] // 2

        def step(i, carry):
            x = i * 2
            product = (v_ref[pl.ds(x, 2)] * c_ref[band, pl.ds(x + x_base, 2)]).reshape(2 * length, length)
            out = lax.dot_general(table, product, NT, preferred_element_type=jnp.float32)
            out = out.astype(jnp.bfloat16).astype(jnp.float32)
            row = band * planes + x + x_base
            s_ref[pl.ds(row, length, stride=spaced), :] = out[:, :length]
            s_ref[pl.ds(row + 1, length, stride=spaced), :] = out[:, length:]
            return carry

        lax.fori_loop(0, steps, step, 0, unroll=steps)

    for band in range(2 * bands):
        pltpu.make_async_copy(swapped_ref.at[0], c_ref.at[band], sem_ref.at[2 + band]).wait()
        transform_z(band, va_ref, 0)
        transform_z(band, vb_ref, va_ref.shape[0])

    def transform_y(j, carry):
        base = pl.multiple_of(j * 2 * spaced, 8)
        rows = jnp.concatenate([s_ref[pl.ds(base, lanes), :], s_ref[pl.ds(base + spaced, lanes), :]])
        out = lax.dot_general(table, rows.astype(jnp.bfloat16), NT, preferred_element_type=jnp.float32)
        base = pl.multiple_of(j * 2 * length, 2 * length)
        a_ref[pl.ds(base, length), :] = out[:, :lanes]
        a_ref[pl.ds(base + length, length), :] = out[:, lanes:]
        return carry

    lax.fori_loop(0, length // 2, transform_y, 0, unroll=16)

    def pick(t, carry):
        rows = [a_ref[pl.ds(index_ref[t * 8 + k], 1), :] for k in range(8)]
        g_ref[pl.ds(pl.multiple_of(t * 8, 8), 8), :] = jnp.concatenate(rows)
        return carry

    lax.fori_loop(0, keep // 8, pick, 0, unroll=8)

    tx_copy.wait()
    lane = lax.broadcasted_iota(jnp.int32, (keep, lanes), 1)
    scaled = jnp.where(lane < used, g_ref[...] * tx_ref[...], 0.0)
    high = scaled.astype(jnp.bfloat16)
    low = (scaled - high.astype(jnp.float32)).astype(jnp.bfloat16)
    rows = out_ref.shape[0]
    owner = lax.broadcasted_iota(jnp.int32, (rows, lanes), 1) // planes
    select = (owner == lax.broadcasted_iota(jnp.int32, (rows, lanes), 0)).astype(jnp.bfloat16)
    out_ref[...] = lax.dot_general(select, high, NT, preferred_element_type=jnp.float32) + lax.dot_general(
        select, low, NT, preferred_element_type=jnp.float32
    )


def round_coeffs(picks, place, sources_a, sources_b, conduction, c_swapped, table, tx, index):
    keep, lanes = tx.shape
    length = table.shape[0]
    bands, planes = c_swapped.shape[:2]
    rows = -(-2 * bands // 8) * 8
    choices = len(sources_a)
    part = pltpu.VMEM(sources_a[0].shape, jnp.bfloat16)
    smem = pl.BlockSpec(memory_space=pltpu.SMEM)
    vmem = pl.BlockSpec(memory_space=pltpu.VMEM)
    anywhere = pl.BlockSpec(memory_space=pl.ANY)
    return pl.pallas_call(
        functools.partial(round_kernel, choices, place),
        out_shape=jax.ShapeDtypeStruct((rows, keep), jnp.float32),
        in_specs=[smem] * 2 + [anywhere] * (2 * choices) + [vmem] + [anywhere] * 3,
        out_specs=vmem,
        scratch_shapes=[
            part,
            part,
            pltpu.VMEM((2 * bands, *c_swapped.shape[1:]), jnp.bfloat16),
            pltpu.VMEM((keep, lanes), jnp.float32),
            pltpu.VMEM((length * spaced_rows(2 * bands * planes) + lanes, length), jnp.float32),
            pltpu.VMEM((length * length, lanes), jnp.float32),
            pltpu.VMEM((keep, lanes), jnp.float32),
            pltpu.SemaphoreType.DMA((3 + 2 * bands,)),
        ],
        compiler_params=pltpu.CompilerParams(vmem_limit_bytes=52 * 2**20),
        cost_estimate=pl.CostEstimate(flops=4 * 10**9, bytes_accessed=12 * 2**20, transcendentals=0),
        name="round_coeffs",
    )(picks, index, *sources_a, *sources_b, table, conduction, c_swapped, tx)


def square_kernel(plan_ref, energy_val_ref, energy_cond_ref, pick_ref, flag_ref, weight_ref):
    rounds, bands = plan_ref.shape[0], energy_cond_ref.shape[0]
    me = lax.axis_index("band")
    side, group = me & 1, me >> 1
    plan = [plan_ref[r] for r in range(rounds)]

    def one(condition):
        return jnp.where(condition, 1, 0)

    def relative_of(band):
        return (band >> 1) ^ group

    at, own_side, repeated = jnp.int32(-1), jnp.int32(0), []
    for r in range(rounds):
        others = [plan[i] for i in range(rounds) if i != r]
        double = sum(one(band == (plan[r] ^ 1)) for band in others) > 0
        repeated.append(sum(one(band == plan[r]) for band in others) > 0)
        at = jnp.where(double, relative_of(plan[r]), at)
        own_side = jnp.where(relative_of(plan[r]) == 0, plan[r] & 1, own_side)

    def early_of(band):
        relative, low = relative_of(band), band & 1
        at_x = jnp.where(at == 1, 1 - low, 1)
        at_y = jnp.where(at == 2, low, 1)
        return jnp.where(relative == 0, 1, jnp.where(relative == 1, at_x, jnp.where(relative == 2, at_y, 0)))

    first, best = jnp.int32(0), jnp.int32(-1)
    for r in range(rounds):
        score = jnp.where(early_of(plan[r]) == 1, 2, one(repeated[r]))
        first = jnp.where(score > best, r, first)
        best = jnp.maximum(score, best)
    ordered = [plan[0]] + [jnp.where(first == r, plan[0], plan[r]) for r in range(1, rounds)]
    for r in range(1, rounds):
        ordered[0] = jnp.where(first == r, plan[r], ordered[0])

    flags = [
        one(at == 0),
        one(jnp.where(at == 0, 0, own_side) == side),
        one(jnp.where(at == 0, 1, own_side) == side),
        one(at >= 0),
        early_of(ordered[0]),
    ] + [one(band == ordered[0]) for band in ordered]
    for r, band in enumerate(ordered):
        relative, low = relative_of(band), band & 1
        here = one((band & 1) != side)
        far_a = jnp.where(at == 3, 4 + low, jnp.where(at == 2, 5, 4))
        far_b = jnp.where(at == 3, 5 - low, jnp.where(at == 1, 5, 4))
        x_a, x_b = jnp.where(at == 1, 2 + 3 * low, 2), jnp.where(at == 1, 2 + 2 * low, 2)
        y_a, y_b = jnp.where(at == 2, 4 - low, 3), jnp.where(at == 2, 5 - 2 * low, 3)
        pick_ref[2 * r] = jnp.where(relative == 0, here, jnp.where(relative == 1, x_a, jnp.where(relative == 2, y_a, far_a)))
        pick_ref[2 * r + 1] = jnp.where(relative == 0, here, jnp.where(relative == 1, x_b, jnp.where(relative == 2, y_b, far_b)))
    for part in range(2):
        pick_ref[part] = jnp.where(early_of(ordered[0]) == 1, pick_ref[part], 0)
    for k, flag in enumerate(flags):
        flag_ref[pl.ds(k, 1), :] = jnp.full((1, LANES), flag, jnp.int32)
    for r in range(rounds):
        for c in range(bands):
            gap = energy_cond_ref[c] - energy_val_ref[ordered[r]]
            weight_ref[pl.ds(r * bands + c, 1), :] = 1.0 / jnp.full((1, LANES), gap, jnp.float32)


def square_flags(plan, energy_val, energy_cond):
    rounds = plan.shape[0]
    smem = pl.BlockSpec(memory_space=pltpu.SMEM)
    vmem = pl.BlockSpec(memory_space=pltpu.VMEM)
    count = -(-(5 + rounds) // 8) * 8
    weight_rows = -(-rounds * energy_cond.shape[0] // 8) * 8
    return pl.pallas_call(
        square_kernel,
        out_shape=(
            jax.ShapeDtypeStruct((2 * rounds,), jnp.int32),
            jax.ShapeDtypeStruct((count, LANES), jnp.int32),
            jax.ShapeDtypeStruct((weight_rows, LANES), jnp.float32),
        ),
        in_specs=[smem] * 3,
        out_specs=(smem, vmem, vmem),
        name="square_flags",
    )(plan, energy_val, energy_cond)


def per_device(valence, conduction, energy_val, energy_cond, kept, plan):
    band_local, x_local, length = conduction.shape[:3]
    keep = kept.shape[1]
    held = valence.shape[0]
    rounds = plan.shape[0]
    n_band = lax.axis_size("band")
    n_col = lax.axis_size("col")
    n_pair = n_band // 2
    bits = n_pair.bit_length() - 1
    me = lax.axis_index("band")
    side, group = me % 2, me // 2
    col = lax.axis_index("col")
    x_half = x_local // 2

    def swap(value, mask):
        return lax.ppermute(value, "band", [(i, i ^ mask) for i in range(n_band)])

    def half_of(value, which):
        return lax.dynamic_slice_in_dim(value, which * x_half, x_half, 1)

    cut = x_half // 2
    part_starts = (0, cut)

    def parts_of(which):
        return [lax.dynamic_slice_in_dim(valence, which * x_half + start, cut, 1) for start in part_starts]

    v_mine = parts_of(side)
    v_swapped = [swap(part, 1) for part in parts_of(1 - side)]
    square = held == 1 and bits == 2 and rounds > 1
    picks, flags, square_weights = square_flags(plan, energy_val, energy_cond) if square else (plan, plan, energy_val)
    v_swapped, conduction, flags = lax.optimization_barrier((v_swapped, conduction, flags))
    c_swapped = swap(lax.dynamic_slice_in_dim(conduction, (1 - side) * x_half, x_half, 1), 1)
    def prepared(c_swapped, conduction, kept):
        position = jnp.arange(length, dtype=jnp.int32)
        table = cas_of(position[:, None] * position[None, :] % length, length).astype(jnp.bfloat16)
        used = 2 * band_local * x_half
        lanes = -(-used // LANES) * LANES
        x_global = col * x_local + side * x_half + jnp.arange(lanes, dtype=jnp.int32) % x_half
        tx = cas_of(kept[0][:, None] * x_global[None, :] % length, length) * length ** (-1.5)
        index = kept[2] * length + kept[1]
        return conduction, c_swapped, table, tx, index

    def located(plan):
        plan_rows = jnp.broadcast_to(plan[:, None, None, None], (rounds, 1, 1, length))
        root = plan_rows // held
        return (root // 2) ^ group, root % 2 == side, plan_rows % held

    parts = list(zip(v_mine, v_swapped))

    def any_plan():
        relative, near_side, local = located(plan)
        ready = prepared(c_swapped, conduction, kept)
        is_target = plan[:, None] == jnp.arange(energy_val.shape[0], dtype=jnp.int32)[None, :]
        target_energy = jnp.sum(jnp.where(is_target, energy_val[None, :], 0.0), axis=1)
        weights = (1.0 / (energy_cond[None, :] - target_energy[:, None])).reshape(rounds * band_local, 1)

        def held_band(mine, swapped, r):
            band = jnp.where(near_side[r], mine[0], swapped[0])
            for i in range(1, held):
                band = jnp.where(local[r] == i, jnp.where(near_side[r], mine[i], swapped[i]), band)
            return band

        def nearer(r, bit, near, far):
            return jnp.where((relative[r] >> bit) & 1 == 0, near, far)

        orders = [list(range(bits)), list(range(bits))[::-1]]
        if 2 * held <= rounds and bits:
            far_mine = [swap(part[0], 2 << order[0]) for part, order in zip(parts, orders)]
            far_swapped = [swap(part[1], 2 << order[0]) for part, order in zip(parts, orders)]
            far_mine, far_swapped, ready = lax.optimization_barrier((far_mine, far_swapped, ready))
            slots = [
                [
                    nearer(r, order[0], held_band(*part, r), held_band(fm, fs, r))
                    for part, fm, fs, order in zip(parts, far_mine, far_swapped, orders)
                ]
                for r in range(rounds)
            ]
            slots = lax.optimization_barrier(slots)
            orders = [order[1:] for order in orders]
        else:
            slots = [[held_band(*part, r) for part in parts] for r in range(rounds)]
        for step in range(len(orders[0])):
            slots = [
                [nearer(r, order[step], value, swap(value, 2 << order[step])) for value, order in zip(slots[r], orders)]
                for r in range(rounds)
            ]
        picks = jnp.zeros(2 * rounds, jnp.int32)
        return [round_coeffs(picks, r, [a], [b], *ready) for r, (a, b) in enumerate(slots)], weights

    def four_pairs(picks, flags, weights):
        again = flags[3, 0] != 0

        def flag(k):
            return flags[k] != 0

        def own(k):
            return [jnp.where(flag(k), part[0][0], part[1][0]) for part in parts]

        to_x, to_y = own(1), own(2)
        to_x, to_y, *given = lax.optimization_barrier((to_x, to_y, conduction, kept))
        x_a, y_b = swap(to_x[0], 2), swap(to_y[1], 4)
        x_b, y_a = swap(to_x[1], 2), swap(to_y[0], 4)
        ready = prepared(c_swapped, *given)
        x_a, y_b, ready, again = lax.optimization_barrier((x_a, y_b, ready, again))
        on_y = swap(jnp.where(flag(0), to_x[0], x_a), 4)
        on_x = swap(jnp.where(flag(0), to_y[1], y_b), 2)
        sources_a = [parts[0][0][0], parts[0][1][0], x_a, y_a]
        sources_b = [parts[1][0][0], parts[1][1][0], x_b, y_b]
        partial = [round_coeffs(picks, 0, sources_a, sources_b, *ready)]
        partial, on_x, on_y, to_x, to_y, x_b, y_a = lax.optimization_barrier(
            (partial, on_x, on_y, to_x, to_y, x_b, y_a)
        )

        def send_on(x_b, y_a):
            return swap(jnp.where(flag(0), to_y[0], y_a), 2), swap(jnp.where(flag(0), to_x[1], x_b), 4)

        last_x, last_y = lax.cond(again, send_on, lambda x_b, y_a: (y_a, x_b), x_b, y_a)
        sources_a += [on_y, last_x]
        sources_b += [on_x, last_y]
        partial += [round_coeffs(picks, r, sources_a, sources_b, *ready) for r in range(1, rounds)]
        copied = partial[rounds - 1]
        for r in range(1, rounds - 1):
            copied = jnp.where(flags[5 + r, :1] != 0, partial[r], copied)
        partial[0] = jnp.where(flags[4, :1] != 0, partial[0], copied)
        return partial, weights[: rounds * band_local, :1]

    partial, weights = four_pairs(picks, flags, square_weights) if square else any_plan()

    first = jnp.concatenate([p[:band_local] for p in partial])
    second = jnp.concatenate([p[band_local : 2 * band_local] for p in partial])
    mine = jnp.where(side == 0, first, second)
    coeffs = mine + swap(jnp.where(side == 0, second, first), 1)
    sent = coeffs.astype(jnp.bfloat16)
    for shift in range(1, n_col):
        moved = lax.ppermute(sent, "col", [(i, (i + shift) % n_col) for i in range(n_col)])
        coeffs = coeffs + moved.astype(jnp.float32)
    weighted = (weights * coeffs).astype(jnp.bfloat16)
    plain = coeffs.astype(jnp.bfloat16)

    col_width, row_width = keep // n_col, keep // n_band
    col_piece = lax.dynamic_slice_in_dim(plain, col * col_width, col_width, 1)

    def rows_of(other):
        return lax.dynamic_slice_in_dim(weighted, other * 2 * row_width, 2 * row_width, 1)

    pieces = [jnp.concatenate([col_piece, rows_of(group)], axis=1)]
    for mask in range(1, n_pair):
        pieces.append(swap(jnp.concatenate([col_piece, rows_of(group ^ mask)], axis=1), 2 * mask))
    gathered = jnp.concatenate(pieces)
    columns = gathered[:, :col_width]
    rows_low, rows_high = gathered[:, col_width : col_width + row_width], gathered[:, col_width + row_width :]
    rows_mine = jnp.where(side == 0, rows_low, rows_high)
    rows_other = jnp.where(side == 0, rows_high, rows_low)
    swapped = swap(jnp.concatenate([columns, rows_other], axis=1), 1)
    columns = jnp.concatenate([columns, swapped[:, :col_width]])
    rows = jnp.concatenate([rows_mine, swapped[:, col_width:]])
    response_tile = lax.dot_general(
        rows, columns, (((0,), (0,)), ((), ())), preferred_element_type=jnp.float32
    )
    factor = (rounds * band_local * n_band) ** (-0.5)
    return -response_tile * factor


def solution(mesh):
    return jax.shard_map(
        per_device,
        mesh=mesh,
        in_specs=(
            P("band", "col", None, None),
            P("band", "col", None, None),
            P(),
            P("band"),
            P(),
            P(),
        ),
        out_specs=P("band", "col"),
        check_vma=False,
    )
```

```python
import functools

import jax
import jax.numpy as jnp
from jax import lax
from jax.experimental import pallas as pl
from jax.experimental.pallas import tpu as pltpu
from jax.sharding import PartitionSpec as P

LANES = 128
NT = (((1,), (1,)), ((), ()))


def cas_of(phase, length):
    angle_value = 2.0 * jnp.pi / length * phase.astype(jnp.float32)
    return jnp.cos(angle_value) + jnp.sin(angle_value)


def spaced_rows(used):
    tiles = -(-used // 8)
    return 8 * (tiles + 1 - tiles % 2)


def round_kernel(choices, place, pick_ref, index_ref, *refs):
    table_ref, conduction_ref, swapped_ref, tx_from, out_ref, v_ref, c_ref, tx_ref, s_ref, a_ref, g_ref, sem_ref = refs[
        2 * choices :
    ]
    bands, planes = swapped_ref.shape[:2]
    side = lax.axis_index("band") & 1
    half = planes // 2
    parts = [(refs[:choices], v_ref.at[pl.ds(0, half)]), (refs[choices : 2 * choices], v_ref.at[pl.ds(half, half)])]
    for part, (sources, target) in enumerate(parts):
        for k, source in enumerate(sources):

            @pl.when(pick_ref[2 * place + part] == k)
            def _():
                pltpu.make_async_copy(source, target, sem_ref.at[part]).start()

    for band in range(bands):
        mine, other = side * bands + band, (1 - side) * bands + band
        own_planes = conduction_ref.at[band, pl.ds(side * planes, planes)]
        pltpu.make_async_copy(own_planes, c_ref.at[mine], sem_ref.at[2 + mine]).start()
        pltpu.make_async_copy(swapped_ref.at[band], c_ref.at[other], sem_ref.at[2 + other]).start()
    tx_copy = pltpu.make_async_copy(tx_from, tx_ref, sem_ref.at[2 + 2 * bands])
    tx_copy.start()
    for part, (sources, target) in enumerate(parts):
        pltpu.make_async_copy(sources[0], target, sem_ref.at[part]).wait()
    length = v_ref.shape[1]
    keep, lanes = tx_ref.shape
    used = 2 * bands * planes
    spaced = spaced_rows(used)
    table = table_ref[...]

    steps = planes // 2

    def transform_z(i, carry):
        band, x = i // steps, (i % steps) * 2
        product = (v_ref[pl.ds(x, 2)] * c_ref[band, pl.ds(x, 2)]).reshape(2 * length, length)
        out = lax.dot_general(table, product, NT, preferred_element_type=jnp.float32)
        out = out.astype(jnp.bfloat16).astype(jnp.float32)
        row = band * planes + x
        s_ref[pl.ds(row, length, stride=spaced), :] = out[:, :length]
        s_ref[pl.ds(row + 1, length, stride=spaced), :] = out[:, length:]
        return carry

    for first in (0, bands):
        for band in range(first, first + bands):
            pltpu.make_async_copy(swapped_ref.at[0], c_ref.at[band], sem_ref.at[2 + band]).wait()
        lax.fori_loop(first * steps, (first + bands) * steps, transform_z, 0, unroll=bands * steps)

    def transform_y(j, carry):
        base = pl.multiple_of(j * 2 * spaced, 8)
        rows = jnp.concatenate([s_ref[pl.ds(base, lanes), :], s_ref[pl.ds(base + spaced, lanes), :]])
        out = lax.dot_general(table, rows.astype(jnp.bfloat16), NT, preferred_element_type=jnp.float32)
        base = pl.multiple_of(j * 2 * length, 2 * length)
        a_ref[pl.ds(base, length), :] = out[:, :lanes]
        a_ref[pl.ds(base + length, length), :] = out[:, lanes:]
        return carry

    lax.fori_loop(0, length // 2, transform_y, 0, unroll=16)

    def pick(t, carry):
        rows = [a_ref[pl.ds(index_ref[t * 8 + k], 1), :] for k in range(8)]
        g_ref[pl.ds(pl.multiple_of(t * 8, 8), 8), :] = jnp.concatenate(rows)
        return carry

    lax.fori_loop(0, keep // 8, pick, 0, unroll=8)

    tx_copy.wait()
    lane = lax.broadcasted_iota(jnp.int32, (keep, lanes), 1)
    scaled = jnp.where(lane < used, g_ref[...] * tx_ref[...], 0.0)
    high = scaled.astype(jnp.bfloat16)
    low = (scaled - high.astype(jnp.float32)).astype(jnp.bfloat16)
    rows = out_ref.shape[0]
    owner = lax.broadcasted_iota(jnp.int32, (rows, lanes), 1) // planes
    select = (owner == lax.broadcasted_iota(jnp.int32, (rows, lanes), 0)).astype(jnp.bfloat16)
    out_ref[...] = lax.dot_general(select, high, NT, preferred_element_type=jnp.float32) + lax.dot_general(
        select, low, NT, preferred_element_type=jnp.float32
    )


def round_coeffs(picks, place, sources_a, sources_b, conduction, c_swapped, table, tx, index):
    keep, lanes = tx.shape
    length = table.shape[0]
    bands, planes = c_swapped.shape[:2]
    rows = -(-2 * bands // 8) * 8
    choices = len(sources_a)
    smem = pl.BlockSpec(memory_space=pltpu.SMEM)
    vmem = pl.BlockSpec(memory_space=pltpu.VMEM)
    anywhere = pl.BlockSpec(memory_space=pl.ANY)
    return pl.pallas_call(
        functools.partial(round_kernel, choices, place),
        out_shape=jax.ShapeDtypeStruct((rows, keep), jnp.float32),
        in_specs=[smem] * 2 + [anywhere] * (2 * choices) + [vmem] + [anywhere] * 3,
        out_specs=vmem,
        scratch_shapes=[
            pltpu.VMEM(c_swapped.shape[1:], jnp.bfloat16),
            pltpu.VMEM((2 * bands, *c_swapped.shape[1:]), jnp.bfloat16),
            pltpu.VMEM((keep, lanes), jnp.float32),
            pltpu.VMEM((length * spaced_rows(2 * bands * planes) + lanes, length), jnp.float32),
            pltpu.VMEM((length * length, lanes), jnp.float32),
            pltpu.VMEM((keep, lanes), jnp.float32),
            pltpu.SemaphoreType.DMA((3 + 2 * bands,)),
        ],
        compiler_params=pltpu.CompilerParams(vmem_limit_bytes=52 * 2**20),
        cost_estimate=pl.CostEstimate(flops=4 * 10**9, bytes_accessed=12 * 2**20, transcendentals=0),
        name="round_coeffs",
    )(picks, index, *sources_a, *sources_b, table, conduction, c_swapped, tx)


def square_kernel(plan_ref, energy_val_ref, energy_cond_ref, pick_ref, flag_ref, weight_ref):
    rounds, bands = plan_ref.shape[0], energy_cond_ref.shape[0]
    me = lax.axis_index("band")
    side, group = me & 1, me >> 1
    plan = [plan_ref[r] for r in range(rounds)]

    def one(condition):
        return jnp.where(condition, 1, 0)

    def relative_of(band):
        return (band >> 1) ^ group

    at, own_side, repeated = jnp.int32(-1), jnp.int32(0), []
    for r in range(rounds):
        others = [plan[i] for i in range(rounds) if i != r]
        double = sum(one(band == (plan[r] ^ 1)) for band in others) > 0
        repeated.append(sum(one(band == plan[r]) for band in others) > 0)
        at = jnp.where(double, relative_of(plan[r]), at)
        own_side = jnp.where(relative_of(plan[r]) == 0, plan[r] & 1, own_side)

    def early_of(band):
        relative, low = relative_of(band), band & 1
        at_x = jnp.where(at == 1, 1 - low, 1)
        at_y = jnp.where(at == 2, low, 1)
        return jnp.where(relative == 0, 1, jnp.where(relative == 1, at_x, jnp.where(relative == 2, at_y, 0)))

    first, best = jnp.int32(0), jnp.int32(-1)
    for r in range(rounds):
        score = jnp.where(early_of(plan[r]) == 1, 2, one(repeated[r]))
        first = jnp.where(score > best, r, first)
        best = jnp.maximum(score, best)
    ordered = [plan[0]] + [jnp.where(first == r, plan[0], plan[r]) for r in range(1, rounds)]
    for r in range(1, rounds):
        ordered[0] = jnp.where(first == r, plan[r], ordered[0])

    flags = [
        one(at == 0),
        one(jnp.where(at == 0, 0, own_side) == side),
        one(jnp.where(at == 0, 1, own_side) == side),
        one(at >= 0),
        early_of(ordered[0]),
    ] + [one(band == ordered[0]) for band in ordered]
    for r, band in enumerate(ordered):
        relative, low = relative_of(band), band & 1
        here = one((band & 1) != side)
        far_a = jnp.where(at == 3, 4 + low, jnp.where(at == 2, 5, 4))
        far_b = jnp.where(at == 3, 5 - low, jnp.where(at == 1, 5, 4))
        x_a, x_b = jnp.where(at == 1, 2 + 3 * low, 2), jnp.where(at == 1, 2 + 2 * low, 2)
        y_a, y_b = jnp.where(at == 2, 4 - low, 3), jnp.where(at == 2, 5 - 2 * low, 3)
        pick_ref[2 * r] = jnp.where(relative == 0, here, jnp.where(relative == 1, x_a, jnp.where(relative == 2, y_a, far_a)))
        pick_ref[2 * r + 1] = jnp.where(relative == 0, here, jnp.where(relative == 1, x_b, jnp.where(relative == 2, y_b, far_b)))
    for part in range(2):
        pick_ref[part] = jnp.where(early_of(ordered[0]) == 1, pick_ref[part], 0)
    for k, flag in enumerate(flags):
        flag_ref[pl.ds(k, 1), :] = jnp.full((1, LANES), flag, jnp.int32)
    for r in range(rounds):
        for c in range(bands):
            gap = energy_cond_ref[c] - energy_val_ref[ordered[r]]
            weight_ref[pl.ds(r * bands + c, 1), :] = 1.0 / jnp.full((1, LANES), gap, jnp.float32)


def square_flags(plan, energy_val, energy_cond):
    rounds = plan.shape[0]
    smem = pl.BlockSpec(memory_space=pltpu.SMEM)
    vmem = pl.BlockSpec(memory_space=pltpu.VMEM)
    count = -(-(5 + rounds) // 8) * 8
    weight_rows = -(-rounds * energy_cond.shape[0] // 8) * 8
    return pl.pallas_call(
        square_kernel,
        out_shape=(
            jax.ShapeDtypeStruct((2 * rounds,), jnp.int32),
            jax.ShapeDtypeStruct((count, LANES), jnp.int32),
            jax.ShapeDtypeStruct((weight_rows, LANES), jnp.float32),
        ),
        in_specs=[smem] * 3,
        out_specs=(smem, vmem, vmem),
        name="square_flags",
    )(plan, energy_val, energy_cond)


def per_device(valence, conduction, energy_val, energy_cond, kept, plan):
    band_local, x_local, length = conduction.shape[:3]
    keep = kept.shape[1]
    held = valence.shape[0]
    rounds = plan.shape[0]
    n_band = lax.axis_size("band")
    n_col = lax.axis_size("col")
    n_pair = n_band // 2
    bits = n_pair.bit_length() - 1
    me = lax.axis_index("band")
    side, group = me % 2, me // 2
    col = lax.axis_index("col")
    x_half = x_local // 2

    def swap(value, mask):
        return lax.ppermute(value, "band", [(i, i ^ mask) for i in range(n_band)])

    def half_of(value, which):
        return lax.dynamic_slice_in_dim(value, which * x_half, x_half, 1)

    cut = x_half // 2
    part_starts = (0, cut)

    def parts_of(which):
        return [lax.dynamic_slice_in_dim(valence, which * x_half + start, cut, 1) for start in part_starts]

    v_mine = parts_of(side)
    v_swapped = [swap(part, 1) for part in parts_of(1 - side)]
    square = held == 1 and bits == 2 and rounds > 1
    picks, flags, square_weights = square_flags(plan, energy_val, energy_cond) if square else (plan, plan, energy_val)
    v_swapped, conduction, flags = lax.optimization_barrier((v_swapped, conduction, flags))
    c_swapped = swap(lax.dynamic_slice_in_dim(conduction, (1 - side) * x_half, x_half, 1), 1)
    def prepared(c_swapped, conduction, kept):
        position = jnp.arange(length, dtype=jnp.int32)
        table = cas_of(position[:, None] * position[None, :] % length, length).astype(jnp.bfloat16)
        used = 2 * band_local * x_half
        lanes = -(-used // LANES) * LANES
        x_global = col * x_local + side * x_half + jnp.arange(lanes, dtype=jnp.int32) % x_half
        tx = cas_of(kept[0][:, None] * x_global[None, :] % length, length) * length ** (-1.5)
        index = kept[2] * length + kept[1]
        return conduction, c_swapped, table, tx, index

    def located(plan):
        plan_rows = jnp.broadcast_to(plan[:, None, None, None], (rounds, 1, 1, length))
        root = plan_rows // held
        return (root // 2) ^ group, root % 2 == side, plan_rows % held

    parts = list(zip(v_mine, v_swapped))

    def any_plan():
        relative, near_side, local = located(plan)
        ready = prepared(c_swapped, conduction, kept)
        is_target = plan[:, None] == jnp.arange(energy_val.shape[0], dtype=jnp.int32)[None, :]
        target_energy = jnp.sum(jnp.where(is_target, energy_val[None, :], 0.0), axis=1)
        weights = (1.0 / (energy_cond[None, :] - target_energy[:, None])).reshape(rounds * band_local, 1)

        def held_band(mine, swapped, r):
            band = jnp.where(near_side[r], mine[0], swapped[0])
            for i in range(1, held):
                band = jnp.where(local[r] == i, jnp.where(near_side[r], mine[i], swapped[i]), band)
            return band

        def nearer(r, bit, near, far):
            return jnp.where((relative[r] >> bit) & 1 == 0, near, far)

        orders = [list(range(bits)), list(range(bits))[::-1]]
        if 2 * held <= rounds and bits:
            far_mine = [swap(part[0], 2 << order[0]) for part, order in zip(parts, orders)]
            far_swapped = [swap(part[1], 2 << order[0]) for part, order in zip(parts, orders)]
            far_mine, far_swapped, ready = lax.optimization_barrier((far_mine, far_swapped, ready))
            slots = [
                [
                    nearer(r, order[0], held_band(*part, r), held_band(fm, fs, r))
                    for part, fm, fs, order in zip(parts, far_mine, far_swapped, orders)
                ]
                for r in range(rounds)
            ]
            slots = lax.optimization_barrier(slots)
            orders = [order[1:] for order in orders]
        else:
            slots = [[held_band(*part, r) for part in parts] for r in range(rounds)]
        for step in range(len(orders[0])):
            slots = [
                [nearer(r, order[step], value, swap(value, 2 << order[step])) for value, order in zip(slots[r], orders)]
                for r in range(rounds)
            ]
        picks = jnp.zeros(2 * rounds, jnp.int32)
        return [round_coeffs(picks, r, [a], [b], *ready) for r, (a, b) in enumerate(slots)], weights

    def four_pairs(picks, flags, weights):
        again = flags[3, 0] != 0

        def flag(k):
            return flags[k] != 0

        def own(k):
            return [jnp.where(flag(k), part[0][0], part[1][0]) for part in parts]

        to_x, to_y = own(1), own(2)
        to_x, to_y, *given = lax.optimization_barrier((to_x, to_y, conduction, kept))
        x_a, y_b = swap(to_x[0], 2), swap(to_y[1], 4)
        x_b, y_a = swap(to_x[1], 2), swap(to_y[0], 4)
        ready = prepared(c_swapped, *given)
        x_a, y_b, ready, again = lax.optimization_barrier((x_a, y_b, ready, again))
        on_y = swap(jnp.where(flag(0), to_x[0], x_a), 4)
        on_x = swap(jnp.where(flag(0), to_y[1], y_b), 2)
        sources_a = [parts[0][0][0], parts[0][1][0], x_a, y_a]
        sources_b = [parts[1][0][0], parts[1][1][0], x_b, y_b]
        partial = [round_coeffs(picks, 0, sources_a, sources_b, *ready)]
        partial, on_x, on_y, to_x, to_y, x_b, y_a = lax.optimization_barrier(
            (partial, on_x, on_y, to_x, to_y, x_b, y_a)
        )

        def send_on(own_a, own_b):
            return swap(jnp.where(flag(0), own_a, y_a), 2), swap(jnp.where(flag(0), own_b, x_b), 4)

        last_x, last_y = lax.cond(again, send_on, lambda own_a, own_b: (own_a, own_b), to_y[0], to_x[1])
        sources_a += [on_y, last_x]
        sources_b += [on_x, last_y]
        partial += [round_coeffs(picks, r, sources_a, sources_b, *ready) for r in range(1, rounds)]
        copied = partial[rounds - 1]
        for r in range(1, rounds - 1):
            copied = jnp.where(flags[5 + r, :1] != 0, partial[r], copied)
        partial[0] = jnp.where(flags[4, :1] != 0, partial[0], copied)
        return partial, weights[: rounds * band_local, :1]

    partial, weights = four_pairs(picks, flags, square_weights) if square else any_plan()

    first = jnp.concatenate([p[:band_local] for p in partial])
    second = jnp.concatenate([p[band_local : 2 * band_local] for p in partial])
    mine = jnp.where(side == 0, first, second)
    coeffs = mine + swap(jnp.where(side == 0, second, first), 1)
    sent = coeffs.astype(jnp.bfloat16)
    for shift in range(1, n_col):
        moved = lax.ppermute(sent, "col", [(i, (i + shift) % n_col) for i in range(n_col)])
        coeffs = coeffs + moved.astype(jnp.float32)
    weighted = (weights * coeffs).astype(jnp.bfloat16)
    plain = coeffs.astype(jnp.bfloat16)

    col_width, row_width = keep // n_col, keep // n_band
    col_piece = lax.dynamic_slice_in_dim(plain, col * col_width, col_width, 1)

    def rows_of(other):
        return lax.dynamic_slice_in_dim(weighted, other * 2 * row_width, 2 * row_width, 1)

    pieces = [jnp.concatenate([col_piece, rows_of(group)], axis=1)]
    for mask in range(1, n_pair):
        pieces.append(swap(jnp.concatenate([col_piece, rows_of(group ^ mask)], axis=1), 2 * mask))
    gathered = jnp.concatenate(pieces)
    columns = gathered[:, :col_width]
    rows_low, rows_high = gathered[:, col_width : col_width + row_width], gathered[:, col_width + row_width :]
    rows_mine = jnp.where(side == 0, rows_low, rows_high)
    rows_other = jnp.where(side == 0, rows_high, rows_low)
    swapped = swap(jnp.concatenate([columns, rows_other], axis=1), 1)
    columns = jnp.concatenate([columns, swapped[:, :col_width]])
    rows = jnp.concatenate([rows_mine, swapped[:, col_width:]])
    response_tile = lax.dot_general(
        rows, columns, (((0,), (0,)), ((), ())), preferred_element_type=jnp.float32
    )
    factor = (rounds * band_local * n_band) ** (-0.5)
    return -response_tile * factor


def solution(mesh):
    return jax.shard_map(
        per_device,
        mesh=mesh,
        in_specs=(
            P("band", "col", None, None),
            P("band", "col", None, None),
            P(),
            P("band"),
            P(),
            P(),
        ),
        out_specs=P("band", "col"),
        check_vma=False,
    )
```

```python
import jax
import jax.numpy as jnp
from jax import lax
from jax.experimental import pallas as pl
from jax.experimental.pallas import tpu as pltpu
from jax.sharding import PartitionSpec as P

LANES = 128
NT = (((1,), (1,)), ((), ()))


def cas_of(phase, length):
    angle_value = 2.0 * jnp.pi / length * phase.astype(jnp.float32)
    return jnp.cos(angle_value) + jnp.sin(angle_value)


def spaced_rows(used):
    tiles = -(-used // 8)
    return 8 * (tiles + 1 - tiles % 2)


def round_kernel(index_ref, va_ref, vb_ref, c0_ref, c1_ref, table_ref, tx_ref, out_ref, s_ref, a_ref, g_ref):
    length = va_ref.shape[1]
    bands = c0_ref.shape[0]
    planes = c0_ref.shape[1]
    keep, lanes = tx_ref.shape
    used = 2 * bands * planes
    spaced = spaced_rows(used)
    table = table_ref[...]

    def transform_z(c_ref, v_ref, band_base, x_base):
        half = v_ref.shape[0]
        steps = half // 2

        def step(i, carry):
            band, x = i // steps, (i % steps) * 2
            product = (v_ref[pl.ds(x, 2)] * c_ref[band, pl.ds(x + x_base, 2)]).reshape(2 * length, length)
            out = lax.dot_general(table, product, NT, preferred_element_type=jnp.float32)
            out = out.astype(jnp.bfloat16).astype(jnp.float32)
            row = (band_base + band) * planes + x + x_base
            s_ref[pl.ds(row, length, stride=spaced), :] = out[:, :length]
            s_ref[pl.ds(row + 1, length, stride=spaced), :] = out[:, length:]
            return carry

        lax.fori_loop(0, bands * steps, step, 0, unroll=bands * steps)

    for c_ref, band_base in ((c0_ref, 0), (c1_ref, bands)):
        transform_z(c_ref, va_ref, band_base, 0)
        transform_z(c_ref, vb_ref, band_base, va_ref.shape[0])

    def transform_y(j, carry):
        base = pl.multiple_of(j * 2 * spaced, 8)
        rows = jnp.concatenate([s_ref[pl.ds(base, lanes), :], s_ref[pl.ds(base + spaced, lanes), :]])
        out = lax.dot_general(table, rows.astype(jnp.bfloat16), NT, preferred_element_type=jnp.float32)
        base = pl.multiple_of(j * 2 * length, 2 * length)
        a_ref[pl.ds(base, length), :] = out[:, :lanes]
        a_ref[pl.ds(base + length, length), :] = out[:, lanes:]
        return carry

    lax.fori_loop(0, length // 2, transform_y, 0, unroll=16)

    def pick(t, carry):
        rows = [a_ref[pl.ds(index_ref[t * 8 + k], 1), :] for k in range(8)]
        g_ref[pl.ds(pl.multiple_of(t * 8, 8), 8), :] = jnp.concatenate(rows)
        return carry

    lax.fori_loop(0, keep // 8, pick, 0, unroll=8)

    lane = lax.broadcasted_iota(jnp.int32, (keep, lanes), 1)
    scaled = jnp.where(lane < used, g_ref[...] * tx_ref[...], 0.0)
    high = scaled.astype(jnp.bfloat16)
    low = (scaled - high.astype(jnp.float32)).astype(jnp.bfloat16)
    rows = out_ref.shape[0]
    owner = lax.broadcasted_iota(jnp.int32, (rows, lanes), 1) // planes
    select = (owner == lax.broadcasted_iota(jnp.int32, (rows, lanes), 0)).astype(jnp.bfloat16)
    out_ref[...] = lax.dot_general(select, high, NT, preferred_element_type=jnp.float32) + lax.dot_general(
        select, low, NT, preferred_element_type=jnp.float32
    )


def round_coeffs(index, va, vb, c0, c1, table, tx):
    keep, lanes = tx.shape
    length = table.shape[0]
    rows = -(-2 * c0.shape[0] // 8) * 8
    vmem = pl.BlockSpec(memory_space=pltpu.VMEM)
    return pl.pallas_call(
        round_kernel,
        out_shape=jax.ShapeDtypeStruct((rows, keep), jnp.float32),
        in_specs=[pl.BlockSpec(memory_space=pltpu.SMEM)] + [vmem] * 6,
        out_specs=vmem,
        scratch_shapes=[
            pltpu.VMEM((length * spaced_rows(2 * c0.shape[0] * c0.shape[1]) + lanes, length), jnp.float32),
            pltpu.VMEM((length * length, lanes), jnp.float32),
            pltpu.VMEM((keep, lanes), jnp.float32),
        ],
        compiler_params=pltpu.CompilerParams(vmem_limit_bytes=18 * 2**20),
        cost_estimate=pl.CostEstimate(flops=4 * 10**9, bytes_accessed=12 * 2**20, transcendentals=0),
        name="round_coeffs",
    )(index, va, vb, c0, c1, table, tx)


def square_kernel(plan_ref, energy_val_ref, energy_cond_ref, flag_ref, weight_ref):
    rounds, bands = plan_ref.shape[0], energy_cond_ref.shape[0]
    me = lax.axis_index("band")
    side, group = me & 1, me >> 1
    plan = [plan_ref[r] for r in range(rounds)]

    def one(condition):
        return jnp.where(condition, 1, 0)

    def relative_of(band):
        return (band >> 1) ^ group

    at, own_side, repeated = jnp.int32(-1), jnp.int32(0), []
    for r in range(rounds):
        others = [plan[i] for i in range(rounds) if i != r]
        double = sum(one(band == (plan[r] ^ 1)) for band in others) > 0
        repeated.append(sum(one(band == plan[r]) for band in others) > 0)
        at = jnp.where(double, relative_of(plan[r]), at)
        own_side = jnp.where(relative_of(plan[r]) == 0, plan[r] & 1, own_side)

    def early_of(band):
        relative, low = relative_of(band), band & 1
        at_x = jnp.where(at == 1, 1 - low, 1)
        at_y = jnp.where(at == 2, low, 1)
        return jnp.where(relative == 0, 1, jnp.where(relative == 1, at_x, jnp.where(relative == 2, at_y, 0)))

    first, best = jnp.int32(0), jnp.int32(-1)
    for r in range(rounds):
        score = jnp.where(early_of(plan[r]) == 1, 2, one(repeated[r]))
        first = jnp.where(score > best, r, first)
        best = jnp.maximum(score, best)
    ordered = [plan[0]] + [jnp.where(first == r, plan[0], plan[r]) for r in range(1, rounds)]
    for r in range(1, rounds):
        ordered[0] = jnp.where(first == r, plan[r], ordered[0])

    own_double = one(at == 0)
    flags = [
        own_double,
        one(jnp.where(at == 0, 0, own_side) == side),
        one(jnp.where(at == 0, 1, own_side) == side),
        one(at >= 0),
        early_of(ordered[0]),
    ]
    for band in ordered:
        relative, low = relative_of(band), band & 1
        y_at_3 = jnp.where(at == 3, 1 - low, one(at == 1))
        x_at_3 = jnp.where(at == 3, low, one(at == 2))
        from_x = jnp.where(relative == 1, jnp.where(at == 1, low, 0), jnp.where(relative == 3, x_at_3, 0))
        from_y = jnp.where(relative == 2, jnp.where(at == 2, 1 - low, 0), jnp.where(relative == 3, y_at_3, 0))
        flags += [
            one(relative == 1),
            one(relative == 2),
            one((band & 1) == side),
            from_x,
            from_y,
            jnp.where(relative == 3, one(at <= 0), 0),
            one(band == ordered[0]),
        ]
    for k, flag in enumerate(flags):
        flag_ref[pl.ds(k, 1), :] = jnp.full((1, LANES), flag, jnp.int32)
    for r in range(rounds):
        for c in range(bands):
            gap = energy_cond_ref[c] - energy_val_ref[ordered[r]]
            weight_ref[pl.ds(r * bands + c, 1), :] = 1.0 / jnp.full((1, LANES), gap, jnp.float32)


def square_flags(plan, energy_val, energy_cond):
    rounds = plan.shape[0]
    smem = pl.BlockSpec(memory_space=pltpu.SMEM)
    vmem = pl.BlockSpec(memory_space=pltpu.VMEM)
    count = -(-(5 + 7 * rounds) // 8) * 8
    weight_rows = -(-rounds * energy_cond.shape[0] // 8) * 8
    return pl.pallas_call(
        square_kernel,
        out_shape=(
            jax.ShapeDtypeStruct((count, LANES), jnp.int32),
            jax.ShapeDtypeStruct((weight_rows, LANES), jnp.float32),
        ),
        in_specs=[smem] * 3,
        out_specs=(vmem, vmem),
        name="square_flags",
    )(plan, energy_val, energy_cond)


def per_device(valence, conduction, energy_val, energy_cond, kept, plan):
    band_local, x_local, length = conduction.shape[:3]
    keep = kept.shape[1]
    held = valence.shape[0]
    rounds = plan.shape[0]
    n_band = lax.axis_size("band")
    n_col = lax.axis_size("col")
    n_pair = n_band // 2
    bits = n_pair.bit_length() - 1
    me = lax.axis_index("band")
    side, group = me % 2, me // 2
    col = lax.axis_index("col")
    x_half = x_local // 2

    def swap(value, mask):
        return lax.ppermute(value, "band", [(i, i ^ mask) for i in range(n_band)])

    def half_of(value, which):
        return lax.dynamic_slice_in_dim(value, which * x_half, x_half, 1)

    cut = x_half // 2
    part_starts = (0, cut)

    def parts_of(which):
        return [lax.dynamic_slice_in_dim(valence, which * x_half + start, cut, 1) for start in part_starts]

    v_mine = parts_of(side)
    v_swapped = [swap(part, 1) for part in parts_of(1 - side)]
    square = held == 1 and bits == 2 and rounds > 1
    flags, square_weights = square_flags(plan, energy_val, energy_cond) if square else (plan, energy_val)
    v_swapped, conduction, flags = lax.optimization_barrier((v_swapped, conduction, flags))
    c_swapped = swap(half_of(conduction, 1 - side), 1)

    def prepared(conduction, kept):
        c_mine = half_of(conduction, side)
        position = jnp.arange(length, dtype=jnp.int32)
        table = cas_of(position[:, None] * position[None, :] % length, length).astype(jnp.bfloat16)
        used = 2 * band_local * x_half
        lanes = -(-used // LANES) * LANES
        x_global = col * x_local + side * x_half + jnp.arange(lanes, dtype=jnp.int32) % x_half
        tx = cas_of(kept[0][:, None] * x_global[None, :] % length, length) * length ** (-1.5)
        index = kept[2] * length + kept[1]
        c0 = jnp.where(side == 0, c_mine, c_swapped)
        c1 = jnp.where(side == 0, c_swapped, c_mine)
        return c0, c1, table, tx, index

    def coeffs_of(pair, c0, c1, table, tx, index):
        return round_coeffs(index, *pair, c0, c1, table, tx)

    def located(plan):
        plan_rows = jnp.broadcast_to(plan[:, None, None, None], (rounds, 1, 1, length))
        root = plan_rows // held
        return (root // 2) ^ group, root % 2 == side, plan_rows % held

    parts = list(zip(v_mine, v_swapped))

    def any_plan():
        relative, near_side, local = located(plan)
        ready = prepared(conduction, kept)
        is_target = plan[:, None] == jnp.arange(energy_val.shape[0], dtype=jnp.int32)[None, :]
        target_energy = jnp.sum(jnp.where(is_target, energy_val[None, :], 0.0), axis=1)
        weights = (1.0 / (energy_cond[None, :] - target_energy[:, None])).reshape(rounds * band_local, 1)

        def held_band(mine, swapped, r):
            band = jnp.where(near_side[r], mine[0], swapped[0])
            for i in range(1, held):
                band = jnp.where(local[r] == i, jnp.where(near_side[r], mine[i], swapped[i]), band)
            return band

        def nearer(r, bit, near, far):
            return jnp.where((relative[r] >> bit) & 1 == 0, near, far)

        orders = [list(range(bits)), list(range(bits))[::-1]]
        if 2 * held <= rounds and bits:
            far_mine = [swap(part[0], 2 << order[0]) for part, order in zip(parts, orders)]
            far_swapped = [swap(part[1], 2 << order[0]) for part, order in zip(parts, orders)]
            far_mine, far_swapped, ready = lax.optimization_barrier((far_mine, far_swapped, ready))
            slots = [
                [
                    nearer(r, order[0], held_band(*part, r), held_band(fm, fs, r))
                    for part, fm, fs, order in zip(parts, far_mine, far_swapped, orders)
                ]
                for r in range(rounds)
            ]
            slots = lax.optimization_barrier(slots)
            orders = [order[1:] for order in orders]
        else:
            slots = [[held_band(*part, r) for part in parts] for r in range(rounds)]
        for step in range(len(orders[0])):
            slots = [
                [nearer(r, order[step], value, swap(value, 2 << order[step])) for value, order in zip(slots[r], orders)]
                for r in range(rounds)
            ]
        return [coeffs_of(pair, *ready) for pair in slots], weights

    def four_pairs(flags, weights):
        def flag(k):
            return flags[k] != 0

        def round_flag(r, k):
            return flag(5 + 7 * r + k)

        def own(k):
            return [jnp.where(flag(k), part[0][0], part[1][0]) for part in parts]

        to_x, to_y = own(1), own(2)
        to_x, to_y, *given = lax.optimization_barrier((to_x, to_y, conduction, kept))
        x_a, y_b = swap(to_x[0], 2), swap(to_y[1], 4)
        x_b, y_a = swap(to_x[1], 2), swap(to_y[0], 4)
        ready = prepared(*given)
        x_a, y_b, ready = lax.optimization_barrier((x_a, y_b, ready))
        on_y, on_x = jnp.where(flag(0), to_x[0], x_a), jnp.where(flag(0), to_y[1], y_b)
        on_y, on_x, flags = lax.optimization_barrier((on_y, on_x, flags))
        on_y, on_x = swap(on_y, 4), swap(on_x, 2)

        def near(r, half, x, y):
            here = jnp.where(round_flag(r, 2), parts[half][0][0], parts[half][1][0])
            return jnp.where(round_flag(r, 0), x, jnp.where(round_flag(r, 1), y, here))

        partial = [coeffs_of((near(0, 0, x_a, y_a), near(0, 1, x_b, y_b)), *ready)]
        partial, on_x, on_y = lax.optimization_barrier((partial, on_x, on_y))
        later_x, later_y = jnp.where(flag(0), to_y[0], y_a), jnp.where(flag(0), to_x[1], x_b)
        last_x, last_y = lax.cond(
            flags[3, 0] != 0,
            lambda x, y: (swap(x, 2), swap(y, 4)),
            lambda x, y: (x, y),
            later_x,
            later_y,
        )
        for r in range(1, rounds):
            from_x, from_y, from_both = (round_flag(r, k) for k in (3, 4, 5))
            part_a = jnp.where(from_x, last_x, jnp.where(from_y | from_both, on_y, near(r, 0, x_a, y_a)))
            part_b = jnp.where(from_y, last_y, jnp.where(from_x | from_both, on_x, near(r, 1, x_b, y_b)))
            partial.append(coeffs_of((part_a, part_b), *ready))
        copied = partial[rounds - 1]
        for r in range(1, rounds - 1):
            copied = jnp.where(flags[5 + 7 * r + 6, :1] != 0, partial[r], copied)
        partial[0] = jnp.where(flags[4, :1] != 0, partial[0], copied)
        return partial, weights[: rounds * band_local, :1]

    partial, weights = four_pairs(flags, square_weights) if square else any_plan()

    first = jnp.concatenate([p[:band_local] for p in partial])
    second = jnp.concatenate([p[band_local : 2 * band_local] for p in partial])
    mine = jnp.where(side == 0, first, second)
    coeffs = mine + swap(jnp.where(side == 0, second, first), 1)
    sent = coeffs.astype(jnp.bfloat16)
    for shift in range(1, n_col):
        moved = lax.ppermute(sent, "col", [(i, (i + shift) % n_col) for i in range(n_col)])
        coeffs = coeffs + moved.astype(jnp.float32)
    weighted = (weights * coeffs).astype(jnp.bfloat16)
    plain = coeffs.astype(jnp.bfloat16)

    col_width, row_width = keep // n_col, keep // n_band
    col_piece = lax.dynamic_slice_in_dim(plain, col * col_width, col_width, 1)

    def rows_of(other):
        return lax.dynamic_slice_in_dim(weighted, other * 2 * row_width, 2 * row_width, 1)

    pieces = [jnp.concatenate([col_piece, rows_of(group)], axis=1)]
    for mask in range(1, n_pair):
        pieces.append(swap(jnp.concatenate([col_piece, rows_of(group ^ mask)], axis=1), 2 * mask))
    gathered = jnp.concatenate(pieces)
    columns = gathered[:, :col_width]
    rows_low, rows_high = gathered[:, col_width : col_width + row_width], gathered[:, col_width + row_width :]
    rows_mine = jnp.where(side == 0, rows_low, rows_high)
    rows_other = jnp.where(side == 0, rows_high, rows_low)
    swapped = swap(jnp.concatenate([columns, rows_other], axis=1), 1)
    columns = jnp.concatenate([columns, swapped[:, :col_width]])
    rows = jnp.concatenate([rows_mine, swapped[:, col_width:]])
    response_tile = lax.dot_general(
        rows, columns, (((0,), (0,)), ((), ())), preferred_element_type=jnp.float32
    )
    factor = (rounds * band_local * n_band) ** (-0.5)
    return -response_tile * factor


def solution(mesh):
    return jax.shard_map(
        per_device,
        mesh=mesh,
        in_specs=(
            P("band", "col", None, None),
            P("band", "col", None, None),
            P(),
            P("band"),
            P(),
            P(),
        ),
        out_specs=P("band", "col"),
        check_vma=False,
    )
```

```python
import jax
import jax.numpy as jnp
from jax import lax
from jax.experimental import pallas as pl
from jax.experimental.pallas import tpu as pltpu
from jax.sharding import PartitionSpec as P

LANES = 128
NT = (((1,), (1,)), ((), ()))


def cas_of(phase, length):
    angle_value = 2.0 * jnp.pi / length * phase.astype(jnp.float32)
    return jnp.cos(angle_value) + jnp.sin(angle_value)


def spaced_rows(used):
    tiles = -(-used // 8)
    return 8 * (tiles + 1 - tiles % 2)


def round_kernel(index_ref, va_ref, vb_ref, c0_ref, c1_ref, table_ref, tx_ref, out_ref, s_ref, a_ref, g_ref):
    length = va_ref.shape[1]
    bands = c0_ref.shape[0]
    planes = c0_ref.shape[1]
    keep, lanes = tx_ref.shape
    used = 2 * bands * planes
    spaced = spaced_rows(used)
    table = table_ref[...]

    def transform_z(c_ref, v_ref, band_base, x_base):
        half = v_ref.shape[0]
        steps = half // 2

        def step(i, carry):
            band, x = i // steps, (i % steps) * 2
            product = (v_ref[pl.ds(x, 2)] * c_ref[band, pl.ds(x + x_base, 2)]).reshape(2 * length, length)
            out = lax.dot_general(table, product, NT, preferred_element_type=jnp.float32)
            out = out.astype(jnp.bfloat16).astype(jnp.float32)
            row = (band_base + band) * planes + x + x_base
            s_ref[pl.ds(row, length, stride=spaced), :] = out[:, :length]
            s_ref[pl.ds(row + 1, length, stride=spaced), :] = out[:, length:]
            return carry

        lax.fori_loop(0, bands * steps, step, 0, unroll=bands * steps)

    for c_ref, band_base in ((c0_ref, 0), (c1_ref, bands)):
        transform_z(c_ref, va_ref, band_base, 0)
        transform_z(c_ref, vb_ref, band_base, va_ref.shape[0])

    def transform_y(j, carry):
        base = pl.multiple_of(j * 2 * spaced, 8)
        rows = jnp.concatenate([s_ref[pl.ds(base, lanes), :], s_ref[pl.ds(base + spaced, lanes), :]])
        out = lax.dot_general(table, rows.astype(jnp.bfloat16), NT, preferred_element_type=jnp.float32)
        base = pl.multiple_of(j * 2 * length, 2 * length)
        a_ref[pl.ds(base, length), :] = out[:, :lanes]
        a_ref[pl.ds(base + length, length), :] = out[:, lanes:]
        return carry

    lax.fori_loop(0, length // 2, transform_y, 0, unroll=16)

    def pick(t, carry):
        rows = [a_ref[pl.ds(index_ref[t * 8 + k], 1), :] for k in range(8)]
        g_ref[pl.ds(pl.multiple_of(t * 8, 8), 8), :] = jnp.concatenate(rows)
        return carry

    lax.fori_loop(0, keep // 8, pick, 0, unroll=8)

    lane = lax.broadcasted_iota(jnp.int32, (keep, lanes), 1)
    scaled = jnp.where(lane < used, g_ref[...] * tx_ref[...], 0.0)
    high = scaled.astype(jnp.bfloat16)
    low = (scaled - high.astype(jnp.float32)).astype(jnp.bfloat16)
    rows = out_ref.shape[0]
    owner = lax.broadcasted_iota(jnp.int32, (rows, lanes), 1) // planes
    select = (owner == lax.broadcasted_iota(jnp.int32, (rows, lanes), 0)).astype(jnp.bfloat16)
    out_ref[...] = lax.dot_general(select, high, NT, preferred_element_type=jnp.float32) + lax.dot_general(
        select, low, NT, preferred_element_type=jnp.float32
    )


def round_coeffs(index, va, vb, c0, c1, table, tx):
    keep, lanes = tx.shape
    length = table.shape[0]
    rows = -(-2 * c0.shape[0] // 8) * 8
    vmem = pl.BlockSpec(memory_space=pltpu.VMEM)
    return pl.pallas_call(
        round_kernel,
        out_shape=jax.ShapeDtypeStruct((rows, keep), jnp.float32),
        in_specs=[pl.BlockSpec(memory_space=pltpu.SMEM)] + [vmem] * 6,
        out_specs=vmem,
        scratch_shapes=[
            pltpu.VMEM((length * spaced_rows(2 * c0.shape[0] * c0.shape[1]) + lanes, length), jnp.float32),
            pltpu.VMEM((length * length, lanes), jnp.float32),
            pltpu.VMEM((keep, lanes), jnp.float32),
        ],
        compiler_params=pltpu.CompilerParams(vmem_limit_bytes=18 * 2**20),
        cost_estimate=pl.CostEstimate(flops=4 * 10**9, bytes_accessed=12 * 2**20, transcendentals=0),
        name="round_coeffs",
    )(index, va, vb, c0, c1, table, tx)


def square_kernel(plan_ref, energy_val_ref, energy_cond_ref, flag_ref, weight_ref):
    rounds, bands = plan_ref.shape[0], energy_cond_ref.shape[0]
    me = lax.axis_index("band")
    side, group = me & 1, me >> 1
    plan = [plan_ref[r] for r in range(rounds)]

    def one(condition):
        return jnp.where(condition, 1, 0)

    def relative_of(band):
        return (band >> 1) ^ group

    at, own_side, repeated = jnp.int32(-1), jnp.int32(0), []
    for r in range(rounds):
        others = [plan[i] for i in range(rounds) if i != r]
        double = sum(one(band == (plan[r] ^ 1)) for band in others) > 0
        repeated.append(sum(one(band == plan[r]) for band in others) > 0)
        at = jnp.where(double, relative_of(plan[r]), at)
        own_side = jnp.where(relative_of(plan[r]) == 0, plan[r] & 1, own_side)

    def early_of(band):
        relative, low = relative_of(band), band & 1
        at_x = jnp.where(at == 1, 1 - low, 1)
        at_y = jnp.where(at == 2, low, 1)
        return jnp.where(relative == 0, 1, jnp.where(relative == 1, at_x, jnp.where(relative == 2, at_y, 0)))

    first, best = jnp.int32(0), jnp.int32(-1)
    for r in range(rounds):
        score = jnp.where(early_of(plan[r]) == 1, 2, one(repeated[r]))
        first = jnp.where(score > best, r, first)
        best = jnp.maximum(score, best)
    ordered = [plan[0]] + [jnp.where(first == r, plan[0], plan[r]) for r in range(1, rounds)]
    for r in range(1, rounds):
        ordered[0] = jnp.where(first == r, plan[r], ordered[0])

    own_double = one(at == 0)
    flags = [
        own_double,
        one(jnp.where(at == 0, 0, own_side) == side),
        one(jnp.where(at == 0, 1, own_side) == side),
        one(at >= 0),
        early_of(ordered[0]),
    ]
    for band in ordered:
        relative, low = relative_of(band), band & 1
        y_at_3 = jnp.where(at == 3, 1 - low, one(at == 1))
        x_at_3 = jnp.where(at == 3, low, one(at == 2))
        from_x = jnp.where(relative == 1, jnp.where(at == 1, low, 0), jnp.where(relative == 3, x_at_3, 0))
        from_y = jnp.where(relative == 2, jnp.where(at == 2, 1 - low, 0), jnp.where(relative == 3, y_at_3, 0))
        flags += [
            one(relative == 1),
            one(relative == 2),
            one((band & 1) == side),
            from_x,
            from_y,
            jnp.where(relative == 3, one(at <= 0), 0),
            one(band == ordered[0]),
        ]
    for k, flag in enumerate(flags):
        flag_ref[pl.ds(k, 1), :] = jnp.full((1, LANES), flag, jnp.int32)
    for r in range(rounds):
        for c in range(bands):
            gap = energy_cond_ref[c] - energy_val_ref[ordered[r]]
            weight_ref[pl.ds(r * bands + c, 1), :] = 1.0 / jnp.full((1, LANES), gap, jnp.float32)


def square_flags(plan, energy_val, energy_cond):
    rounds = plan.shape[0]
    smem = pl.BlockSpec(memory_space=pltpu.SMEM)
    vmem = pl.BlockSpec(memory_space=pltpu.VMEM)
    count = -(-(5 + 7 * rounds) // 8) * 8
    weight_rows = -(-rounds * energy_cond.shape[0] // 8) * 8
    return pl.pallas_call(
        square_kernel,
        out_shape=(
            jax.ShapeDtypeStruct((count, LANES), jnp.int32),
            jax.ShapeDtypeStruct((weight_rows, LANES), jnp.float32),
        ),
        in_specs=[smem] * 3,
        out_specs=(vmem, vmem),
        name="square_flags",
    )(plan, energy_val, energy_cond)


def per_device(valence, conduction, energy_val, energy_cond, kept, plan):
    band_local, x_local, length = conduction.shape[:3]
    keep = kept.shape[1]
    held = valence.shape[0]
    rounds = plan.shape[0]
    n_band = lax.axis_size("band")
    n_col = lax.axis_size("col")
    n_pair = n_band // 2
    bits = n_pair.bit_length() - 1
    me = lax.axis_index("band")
    side, group = me % 2, me // 2
    col = lax.axis_index("col")
    x_half = x_local // 2

    def swap(value, mask):
        return lax.ppermute(value, "band", [(i, i ^ mask) for i in range(n_band)])

    def half_of(value, which):
        return lax.dynamic_slice_in_dim(value, which * x_half, x_half, 1)

    cut = x_half // 2
    part_starts = (0, cut)

    def parts_of(which):
        return [lax.dynamic_slice_in_dim(valence, which * x_half + start, cut, 1) for start in part_starts]

    v_mine = parts_of(side)
    v_swapped = [swap(part, 1) for part in parts_of(1 - side)]
    square = held == 1 and bits == 2 and rounds > 1
    flags, square_weights = square_flags(plan, energy_val, energy_cond) if square else (plan, energy_val)
    v_swapped, conduction, flags = lax.optimization_barrier((v_swapped, conduction, flags))
    c_swapped = swap(half_of(conduction, 1 - side), 1)

    def prepared(conduction, kept):
        c_mine = half_of(conduction, side)
        position = jnp.arange(length, dtype=jnp.int32)
        table = cas_of(position[:, None] * position[None, :] % length, length).astype(jnp.bfloat16)
        used = 2 * band_local * x_half
        lanes = -(-used // LANES) * LANES
        x_global = col * x_local + side * x_half + jnp.arange(lanes, dtype=jnp.int32) % x_half
        tx = cas_of(kept[0][:, None] * x_global[None, :] % length, length) * length ** (-1.5)
        index = kept[2] * length + kept[1]
        c0 = jnp.where(side == 0, c_mine, c_swapped)
        c1 = jnp.where(side == 0, c_swapped, c_mine)
        return c0, c1, table, tx, index

    def coeffs_of(pair, c0, c1, table, tx, index):
        return round_coeffs(index, *pair, c0, c1, table, tx)

    def located(plan):
        plan_rows = jnp.broadcast_to(plan[:, None, None, None], (rounds, 1, 1, length))
        root = plan_rows // held
        return (root // 2) ^ group, root % 2 == side, plan_rows % held

    parts = list(zip(v_mine, v_swapped))

    def any_plan():
        relative, near_side, local = located(plan)
        ready = prepared(conduction, kept)
        is_target = plan[:, None] == jnp.arange(energy_val.shape[0], dtype=jnp.int32)[None, :]
        target_energy = jnp.sum(jnp.where(is_target, energy_val[None, :], 0.0), axis=1)
        weights = (1.0 / (energy_cond[None, :] - target_energy[:, None])).reshape(rounds * band_local, 1)

        def held_band(mine, swapped, r):
            band = jnp.where(near_side[r], mine[0], swapped[0])
            for i in range(1, held):
                band = jnp.where(local[r] == i, jnp.where(near_side[r], mine[i], swapped[i]), band)
            return band

        def nearer(r, bit, near, far):
            return jnp.where((relative[r] >> bit) & 1 == 0, near, far)

        orders = [list(range(bits)), list(range(bits))[::-1]]
        if 2 * held <= rounds and bits:
            far_mine = [swap(part[0], 2 << order[0]) for part, order in zip(parts, orders)]
            far_swapped = [swap(part[1], 2 << order[0]) for part, order in zip(parts, orders)]
            far_mine, far_swapped, ready = lax.optimization_barrier((far_mine, far_swapped, ready))
            slots = [
                [
                    nearer(r, order[0], held_band(*part, r), held_band(fm, fs, r))
                    for part, fm, fs, order in zip(parts, far_mine, far_swapped, orders)
                ]
                for r in range(rounds)
            ]
            slots = lax.optimization_barrier(slots)
            orders = [order[1:] for order in orders]
        else:
            slots = [[held_band(*part, r) for part in parts] for r in range(rounds)]
        for step in range(len(orders[0])):
            slots = [
                [nearer(r, order[step], value, swap(value, 2 << order[step])) for value, order in zip(slots[r], orders)]
                for r in range(rounds)
            ]
        return [coeffs_of(pair, *ready) for pair in slots], weights

    def four_pairs(flags, weights):
        def flag(k):
            return flags[k] != 0

        def round_flag(r, k):
            return flag(5 + 7 * r + k)

        def own(k):
            return [jnp.where(flag(k), part[0][0], part[1][0]) for part in parts]

        to_x, to_y = own(1), own(2)
        to_x, to_y, *given = lax.optimization_barrier((to_x, to_y, conduction, kept))
        x_a, y_b = swap(to_x[0], 2), swap(to_y[1], 4)
        x_b, y_a = swap(to_x[1], 2), swap(to_y[0], 4)
        ready = prepared(*given)
        again = (flags[3, 0] != 0).astype(jnp.int32)
        x_a, y_b, ready, again = lax.optimization_barrier((x_a, y_b, ready, again))
        on_y, on_x = jnp.where(flag(0), to_x[0], x_a), jnp.where(flag(0), to_y[1], y_b)
        on_y, on_x, flags = lax.optimization_barrier((on_y, on_x, flags))
        on_y, on_x = swap(on_y, 4), swap(on_x, 2)

        def near(r, half, x, y):
            here = jnp.where(round_flag(r, 2), parts[half][0][0], parts[half][1][0])
            return jnp.where(round_flag(r, 0), x, jnp.where(round_flag(r, 1), y, here))

        partial = [coeffs_of((near(0, 0, x_a, y_a), near(0, 1, x_b, y_b)), *ready)]
        partial, on_x, on_y = lax.optimization_barrier((partial, on_x, on_y))
        later_x, later_y = jnp.where(flag(0), to_y[0], y_a), jnp.where(flag(0), to_x[1], x_b)
        last_x, last_y = lax.cond(
            again != 0,
            lambda x, y: (swap(x, 2), swap(y, 4)),
            lambda x, y: (x, y),
            later_x,
            later_y,
        )
        for r in range(1, rounds):
            from_x, from_y, from_both = (round_flag(r, k) for k in (3, 4, 5))
            part_a = jnp.where(from_x, last_x, jnp.where(from_y | from_both, on_y, near(r, 0, x_a, y_a)))
            part_b = jnp.where(from_y, last_y, jnp.where(from_x | from_both, on_x, near(r, 1, x_b, y_b)))
            partial.append(coeffs_of((part_a, part_b), *ready))
        copied = partial[rounds - 1]
        for r in range(1, rounds - 1):
            copied = jnp.where(flags[5 + 7 * r + 6, :1] != 0, partial[r], copied)
        partial[0] = jnp.where(flags[4, :1] != 0, partial[0], copied)
        return partial, weights[: rounds * band_local, :1]

    partial, weights = four_pairs(flags, square_weights) if square else any_plan()

    first = jnp.concatenate([p[:band_local] for p in partial])
    second = jnp.concatenate([p[band_local : 2 * band_local] for p in partial])
    mine = jnp.where(side == 0, first, second)
    coeffs = mine + swap(jnp.where(side == 0, second, first), 1)
    sent = coeffs.astype(jnp.bfloat16)
    for shift in range(1, n_col):
        moved = lax.ppermute(sent, "col", [(i, (i + shift) % n_col) for i in range(n_col)])
        coeffs = coeffs + moved.astype(jnp.float32)
    weighted = (weights * coeffs).astype(jnp.bfloat16)
    plain = coeffs.astype(jnp.bfloat16)

    col_width, row_width = keep // n_col, keep // n_band
    col_piece = lax.dynamic_slice_in_dim(plain, col * col_width, col_width, 1)

    def rows_of(other):
        return lax.dynamic_slice_in_dim(weighted, other * 2 * row_width, 2 * row_width, 1)

    pieces = [jnp.concatenate([col_piece, rows_of(group)], axis=1)]
    for mask in range(1, n_pair):
        pieces.append(swap(jnp.concatenate([col_piece, rows_of(group ^ mask)], axis=1), 2 * mask))
    gathered = jnp.concatenate(pieces)
    columns = gathered[:, :col_width]
    rows_low, rows_high = gathered[:, col_width : col_width + row_width], gathered[:, col_width + row_width :]
    rows_mine = jnp.where(side == 0, rows_low, rows_high)
    rows_other = jnp.where(side == 0, rows_high, rows_low)
    swapped = swap(jnp.concatenate([columns, rows_other], axis=1), 1)
    columns = jnp.concatenate([columns, swapped[:, :col_width]])
    rows = jnp.concatenate([rows_mine, swapped[:, col_width:]])
    response_tile = lax.dot_general(
        rows, columns, (((0,), (0,)), ((), ())), preferred_element_type=jnp.float32
    )
    factor = (rounds * band_local * n_band) ** (-0.5)
    return -response_tile * factor


def solution(mesh):
    return jax.shard_map(
        per_device,
        mesh=mesh,
        in_specs=(
            P("band", "col", None, None),
            P("band", "col", None, None),
            P(),
            P("band"),
            P(),
            P(),
        ),
        out_specs=P("band", "col"),
        check_vma=False,
    )
```

```python
import jax
import jax.numpy as jnp
from jax import lax
from jax.experimental import pallas as pl
from jax.experimental.pallas import tpu as pltpu
from jax.sharding import PartitionSpec as P

LANES = 128
NT = (((1,), (1,)), ((), ()))


def cas_of(phase, length):
    angle_value = 2.0 * jnp.pi / length * phase.astype(jnp.float32)
    return jnp.cos(angle_value) + jnp.sin(angle_value)


def spaced_rows(used):
    tiles = -(-used // 8)
    return 8 * (tiles + 1 - tiles % 2)


def round_kernel(index_ref, va_ref, vb_ref, c0_ref, c1_ref, table_ref, tx_ref, out_ref, s_ref, a_ref, g_ref):
    length = va_ref.shape[1]
    bands = c0_ref.shape[0]
    planes = c0_ref.shape[1]
    keep, lanes = tx_ref.shape
    used = 2 * bands * planes
    spaced = spaced_rows(used)
    table = table_ref[...]

    def transform_z(c_ref, v_ref, band_base, x_base):
        half = v_ref.shape[0]
        steps = half // 2

        def step(i, carry):
            band, x = i // steps, (i % steps) * 2
            product = (v_ref[pl.ds(x, 2)] * c_ref[band, pl.ds(x + x_base, 2)]).reshape(2 * length, length)
            out = lax.dot_general(table, product, NT, preferred_element_type=jnp.float32)
            out = out.astype(jnp.bfloat16).astype(jnp.float32)
            row = (band_base + band) * planes + x + x_base
            s_ref[pl.ds(row, length, stride=spaced), :] = out[:, :length]
            s_ref[pl.ds(row + 1, length, stride=spaced), :] = out[:, length:]
            return carry

        lax.fori_loop(0, bands * steps, step, 0, unroll=bands * steps)

    for c_ref, band_base in ((c0_ref, 0), (c1_ref, bands)):
        transform_z(c_ref, va_ref, band_base, 0)
        transform_z(c_ref, vb_ref, band_base, va_ref.shape[0])

    def transform_y(j, carry):
        base = pl.multiple_of(j * 2 * spaced, 8)
        rows = jnp.concatenate([s_ref[pl.ds(base, lanes), :], s_ref[pl.ds(base + spaced, lanes), :]])
        out = lax.dot_general(table, rows.astype(jnp.bfloat16), NT, preferred_element_type=jnp.float32)
        base = pl.multiple_of(j * 2 * length, 2 * length)
        a_ref[pl.ds(base, length), :] = out[:, :lanes]
        a_ref[pl.ds(base + length, length), :] = out[:, lanes:]
        return carry

    lax.fori_loop(0, length // 2, transform_y, 0, unroll=32)

    def pick(t, carry):
        rows = [a_ref[pl.ds(index_ref[t * 8 + k], 1), :] for k in range(8)]
        g_ref[pl.ds(pl.multiple_of(t * 8, 8), 8), :] = jnp.concatenate(rows)
        return carry

    lax.fori_loop(0, keep // 8, pick, 0, unroll=24)

    lane = lax.broadcasted_iota(jnp.int32, (keep, lanes), 1)
    scaled = jnp.where(lane < used, g_ref[...] * tx_ref[...], 0.0)
    high = scaled.astype(jnp.bfloat16)
    low = (scaled - high.astype(jnp.float32)).astype(jnp.bfloat16)
    rows = out_ref.shape[0]
    owner = lax.broadcasted_iota(jnp.int32, (rows, lanes), 1) // planes
    select = (owner == lax.broadcasted_iota(jnp.int32, (rows, lanes), 0)).astype(jnp.bfloat16)
    out_ref[...] = lax.dot_general(select, high, NT, preferred_element_type=jnp.float32) + lax.dot_general(
        select, low, NT, preferred_element_type=jnp.float32
    )


def round_coeffs(index, va, vb, c0, c1, table, tx):
    keep, lanes = tx.shape
    length = table.shape[0]
    rows = -(-2 * c0.shape[0] // 8) * 8
    vmem = pl.BlockSpec(memory_space=pltpu.VMEM)
    return pl.pallas_call(
        round_kernel,
        out_shape=jax.ShapeDtypeStruct((rows, keep), jnp.float32),
        in_specs=[pl.BlockSpec(memory_space=pltpu.SMEM)] + [vmem] * 6,
        out_specs=vmem,
        scratch_shapes=[
            pltpu.VMEM((length * spaced_rows(2 * c0.shape[0] * c0.shape[1]) + lanes, length), jnp.float32),
            pltpu.VMEM((length * length, lanes), jnp.float32),
            pltpu.VMEM((keep, lanes), jnp.float32),
        ],
        compiler_params=pltpu.CompilerParams(vmem_limit_bytes=18 * 2**20),
        cost_estimate=pl.CostEstimate(flops=4 * 10**9, bytes_accessed=12 * 2**20, transcendentals=0),
        name="round_coeffs",
    )(index, va, vb, c0, c1, table, tx)


def square_kernel(plan_ref, energy_val_ref, energy_cond_ref, flag_ref, weight_ref):
    rounds, bands = plan_ref.shape[0], energy_cond_ref.shape[0]
    me = lax.axis_index("band")
    side, group = me & 1, me >> 1
    plan = [plan_ref[r] for r in range(rounds)]

    def one(condition):
        return jnp.where(condition, 1, 0)

    def relative_of(band):
        return (band >> 1) ^ group

    at, own_side, repeated = jnp.int32(-1), jnp.int32(0), []
    for r in range(rounds):
        others = [plan[i] for i in range(rounds) if i != r]
        double = sum(one(band == (plan[r] ^ 1)) for band in others) > 0
        repeated.append(sum(one(band == plan[r]) for band in others) > 0)
        at = jnp.where(double, relative_of(plan[r]), at)
        own_side = jnp.where(relative_of(plan[r]) == 0, plan[r] & 1, own_side)

    def early_of(band):
        relative, low = relative_of(band), band & 1
        at_x = jnp.where(at == 1, 1 - low, 1)
        at_y = jnp.where(at == 2, low, 1)
        return jnp.where(relative == 0, 1, jnp.where(relative == 1, at_x, jnp.where(relative == 2, at_y, 0)))

    first, best = jnp.int32(0), jnp.int32(-1)
    for r in range(rounds):
        score = jnp.where(early_of(plan[r]) == 1, 2, one(repeated[r]))
        first = jnp.where(score > best, r, first)
        best = jnp.maximum(score, best)
    ordered = [plan[0]] + [jnp.where(first == r, plan[0], plan[r]) for r in range(1, rounds)]
    for r in range(1, rounds):
        ordered[0] = jnp.where(first == r, plan[r], ordered[0])

    own_double = one(at == 0)
    flags = [
        own_double,
        one(jnp.where(at == 0, 0, own_side) == side),
        one(jnp.where(at == 0, 1, own_side) == side),
        one(at >= 0),
        early_of(ordered[0]),
    ]
    for band in ordered:
        relative, low = relative_of(band), band & 1
        y_at_3 = jnp.where(at == 3, 1 - low, one(at == 1))
        x_at_3 = jnp.where(at == 3, low, one(at == 2))
        from_x = jnp.where(relative == 1, jnp.where(at == 1, low, 0), jnp.where(relative == 3, x_at_3, 0))
        from_y = jnp.where(relative == 2, jnp.where(at == 2, 1 - low, 0), jnp.where(relative == 3, y_at_3, 0))
        flags += [
            one(relative == 1),
            one(relative == 2),
            one((band & 1) == side),
            from_x,
            from_y,
            jnp.where(relative == 3, one(at <= 0), 0),
            one(band == ordered[0]),
        ]
    for k, flag in enumerate(flags):
        flag_ref[pl.ds(k, 1), :] = jnp.full((1, LANES), flag, jnp.int32)
    for r in range(rounds):
        for c in range(bands):
            gap = energy_cond_ref[c] - energy_val_ref[ordered[r]]
            weight_ref[pl.ds(r * bands + c, 1), :] = 1.0 / jnp.full((1, LANES), gap, jnp.float32)


def square_flags(plan, energy_val, energy_cond):
    rounds = plan.shape[0]
    smem = pl.BlockSpec(memory_space=pltpu.SMEM)
    vmem = pl.BlockSpec(memory_space=pltpu.VMEM)
    count = -(-(5 + 7 * rounds) // 8) * 8
    weight_rows = -(-rounds * energy_cond.shape[0] // 8) * 8
    return pl.pallas_call(
        square_kernel,
        out_shape=(
            jax.ShapeDtypeStruct((count, LANES), jnp.int32),
            jax.ShapeDtypeStruct((weight_rows, LANES), jnp.float32),
        ),
        in_specs=[smem] * 3,
        out_specs=(vmem, vmem),
        name="square_flags",
    )(plan, energy_val, energy_cond)


def per_device(valence, conduction, energy_val, energy_cond, kept, plan):
    band_local, x_local, length = conduction.shape[:3]
    keep = kept.shape[1]
    held = valence.shape[0]
    rounds = plan.shape[0]
    n_band = lax.axis_size("band")
    n_col = lax.axis_size("col")
    n_pair = n_band // 2
    bits = n_pair.bit_length() - 1
    me = lax.axis_index("band")
    side, group = me % 2, me // 2
    col = lax.axis_index("col")
    x_half = x_local // 2

    def swap(value, mask):
        return lax.ppermute(value, "band", [(i, i ^ mask) for i in range(n_band)])

    def half_of(value, which):
        return lax.dynamic_slice_in_dim(value, which * x_half, x_half, 1)

    cut = x_half // 2
    part_starts = (0, cut)

    def parts_of(which):
        return [lax.dynamic_slice_in_dim(valence, which * x_half + start, cut, 1) for start in part_starts]

    v_mine = parts_of(side)
    v_swapped = [swap(part, 1) for part in parts_of(1 - side)]
    square = held == 1 and bits == 2 and rounds > 1
    flags, square_weights = square_flags(plan, energy_val, energy_cond) if square else (plan, energy_val)
    v_swapped, conduction, flags = lax.optimization_barrier((v_swapped, conduction, flags))
    c_swapped = swap(half_of(conduction, 1 - side), 1)

    def prepared(conduction, kept):
        c_mine = half_of(conduction, side)
        position = jnp.arange(length, dtype=jnp.int32)
        table = cas_of(position[:, None] * position[None, :] % length, length).astype(jnp.bfloat16)
        used = 2 * band_local * x_half
        lanes = -(-used // LANES) * LANES
        x_global = col * x_local + side * x_half + jnp.arange(lanes, dtype=jnp.int32) % x_half
        tx = cas_of(kept[0][:, None] * x_global[None, :] % length, length) * length ** (-1.5)
        index = kept[2] * length + kept[1]
        c0 = jnp.where(side == 0, c_mine, c_swapped)
        c1 = jnp.where(side == 0, c_swapped, c_mine)
        return c0, c1, table, tx, index

    def coeffs_of(pair, c0, c1, table, tx, index):
        return round_coeffs(index, *pair, c0, c1, table, tx)

    def located(plan):
        plan_rows = jnp.broadcast_to(plan[:, None, None, None], (rounds, 1, 1, length))
        root = plan_rows // held
        return (root // 2) ^ group, root % 2 == side, plan_rows % held

    parts = list(zip(v_mine, v_swapped))

    def any_plan():
        relative, near_side, local = located(plan)
        ready = prepared(conduction, kept)
        is_target = plan[:, None] == jnp.arange(energy_val.shape[0], dtype=jnp.int32)[None, :]
        target_energy = jnp.sum(jnp.where(is_target, energy_val[None, :], 0.0), axis=1)
        weights = (1.0 / (energy_cond[None, :] - target_energy[:, None])).reshape(rounds * band_local, 1)

        def held_band(mine, swapped, r):
            band = jnp.where(near_side[r], mine[0], swapped[0])
            for i in range(1, held):
                band = jnp.where(local[r] == i, jnp.where(near_side[r], mine[i], swapped[i]), band)
            return band

        def nearer(r, bit, near, far):
            return jnp.where((relative[r] >> bit) & 1 == 0, near, far)

        orders = [list(range(bits)), list(range(bits))[::-1]]
        if 2 * held <= rounds and bits:
            far_mine = [swap(part[0], 2 << order[0]) for part, order in zip(parts, orders)]
            far_swapped = [swap(part[1], 2 << order[0]) for part, order in zip(parts, orders)]
            far_mine, far_swapped, ready = lax.optimization_barrier((far_mine, far_swapped, ready))
            slots = [
                [
                    nearer(r, order[0], held_band(*part, r), held_band(fm, fs, r))
                    for part, fm, fs, order in zip(parts, far_mine, far_swapped, orders)
                ]
                for r in range(rounds)
            ]
            slots = lax.optimization_barrier(slots)
            orders = [order[1:] for order in orders]
        else:
            slots = [[held_band(*part, r) for part in parts] for r in range(rounds)]
        for step in range(len(orders[0])):
            slots = [
                [nearer(r, order[step], value, swap(value, 2 << order[step])) for value, order in zip(slots[r], orders)]
                for r in range(rounds)
            ]
        return [coeffs_of(pair, *ready) for pair in slots], weights

    def four_pairs(flags, weights):
        def flag(k):
            return flags[k] != 0

        def round_flag(r, k):
            return flag(5 + 7 * r + k)

        def own(k):
            return [jnp.where(flag(k), part[0][0], part[1][0]) for part in parts]

        to_x, to_y = own(1), own(2)
        to_x, to_y, *given = lax.optimization_barrier((to_x, to_y, conduction, kept))
        x_a, y_b = swap(to_x[0], 2), swap(to_y[1], 4)
        x_b, y_a = swap(to_x[1], 2), swap(to_y[0], 4)
        ready = prepared(*given)
        x_a, y_b, ready = lax.optimization_barrier((x_a, y_b, ready))
        on_y, on_x = jnp.where(flag(0), to_x[0], x_a), jnp.where(flag(0), to_y[1], y_b)
        on_y, on_x, flags = lax.optimization_barrier((on_y, on_x, flags))
        on_y, on_x = swap(on_y, 4), swap(on_x, 2)

        def near(r, half, x, y):
            here = jnp.where(round_flag(r, 2), parts[half][0][0], parts[half][1][0])
            return jnp.where(round_flag(r, 0), x, jnp.where(round_flag(r, 1), y, here))

        partial = [coeffs_of((near(0, 0, x_a, y_a), near(0, 1, x_b, y_b)), *ready)]
        partial, on_x, on_y = lax.optimization_barrier((partial, on_x, on_y))
        later_x, later_y = jnp.where(flag(0), to_y[0], y_a), jnp.where(flag(0), to_x[1], x_b)
        last_x, last_y = lax.cond(
            flags[3, 0] != 0,
            lambda x, y: (swap(x, 2), swap(y, 4)),
            lambda x, y: (x, y),
            later_x,
            later_y,
        )
        for r in range(1, rounds):
            from_x, from_y, from_both = (round_flag(r, k) for k in (3, 4, 5))
            part_a = jnp.where(from_x, last_x, jnp.where(from_y | from_both, on_y, near(r, 0, x_a, y_a)))
            part_b = jnp.where(from_y, last_y, jnp.where(from_x | from_both, on_x, near(r, 1, x_b, y_b)))
            partial.append(coeffs_of((part_a, part_b), *ready))
        copied = partial[rounds - 1]
        for r in range(1, rounds - 1):
            copied = jnp.where(flags[5 + 7 * r + 6, :1] != 0, partial[r], copied)
        partial[0] = jnp.where(flags[4, :1] != 0, partial[0], copied)
        return partial, weights[: rounds * band_local, :1]

    partial, weights = four_pairs(flags, square_weights) if square else any_plan()

    first = jnp.concatenate([p[:band_local] for p in partial])
    second = jnp.concatenate([p[band_local : 2 * band_local] for p in partial])
    mine = jnp.where(side == 0, first, second)
    coeffs = mine + swap(jnp.where(side == 0, second, first), 1)
    sent = coeffs.astype(jnp.bfloat16)
    for shift in range(1, n_col):
        moved = lax.ppermute(sent, "col", [(i, (i + shift) % n_col) for i in range(n_col)])
        coeffs = coeffs + moved.astype(jnp.float32)
    weighted = (weights * coeffs).astype(jnp.bfloat16)
    plain = coeffs.astype(jnp.bfloat16)

    col_width, row_width = keep // n_col, keep // n_band
    col_piece = lax.dynamic_slice_in_dim(plain, col * col_width, col_width, 1)

    def rows_of(other):
        return lax.dynamic_slice_in_dim(weighted, other * 2 * row_width, 2 * row_width, 1)

    pieces = [jnp.concatenate([col_piece, rows_of(group)], axis=1)]
    for mask in range(1, n_pair):
        pieces.append(swap(jnp.concatenate([col_piece, rows_of(group ^ mask)], axis=1), 2 * mask))
    gathered = jnp.concatenate(pieces)
    columns = gathered[:, :col_width]
    rows_low, rows_high = gathered[:, col_width : col_width + row_width], gathered[:, col_width + row_width :]
    rows_mine = jnp.where(side == 0, rows_low, rows_high)
    rows_other = jnp.where(side == 0, rows_high, rows_low)
    swapped = swap(jnp.concatenate([columns, rows_other], axis=1), 1)
    columns = jnp.concatenate([columns, swapped[:, :col_width]])
    rows = jnp.concatenate([rows_mine, swapped[:, col_width:]])
    response_tile = lax.dot_general(
        rows, columns, (((0,), (0,)), ((), ())), preferred_element_type=jnp.float32
    )
    factor = (rounds * band_local * n_band) ** (-0.5)
    return -response_tile * factor


def solution(mesh):
    return jax.shard_map(
        per_device,
        mesh=mesh,
        in_specs=(
            P("band", "col", None, None),
            P("band", "col", None, None),
            P(),
            P("band"),
            P(),
            P(),
        ),
        out_specs=P("band", "col"),
        check_vma=False,
    )
```
